256 devices in a mesh: slab: 32 (over y, z_lo, core), chan: 8 (over z_hi, x).
Axes of the slice: x: 4, y: 4, z: 8 (z_hi: 2, z_lo: 4; z = z_hi * 4 + z_lo), core: 2. Of those that a mesh axis runs over, the one named last changes fastest.
Arguments:
- iterate: bfloat16 [24576, 4096], P('chan', 'slab'), may hold values from -6 to 6
- source: bfloat16 [24576, 4096], P('chan', 'slab'), may hold values from -6 to 6
- coupling: bfloat16 [192, 12, 128, 128], P('chan'), may hold values from -0.15625 to 0.15625
- pair_rows: int32 [192, 12], P('chan'), may hold values from 0 to 191, all different within a row
- diag_pot: float32 [24576, 512], P('chan', 'slab'), may hold values from -2 to 2
- profile: float32 [512], P('slab'), may hold values from 0.3 to 3
- regular: float32 [24576, 512], P('chan', 'slab'), may hold values from -6 to 6
- irregular: float32 [24576, 512], P('chan', 'slab'), may hold values from -6 to 6
Outputs:
- updated: bfloat16 [24576, 4096], P('chan', 'slab')
The draws below stay inside these ranges and needn't reach their ends.
Inputs may be any that keep to these rules, and one draw needn't show every extreme that they name: `pair_rows`: each column block names 12 different row blocks; every row block is named by some column block.
All inputs are finite; a program needn't handle non-finite values.
Results may differ from the reference program's by a relative error of at most 0.001.
Values sent between devices are 32-bit elements; how exact they have to be, the bound alone decides.
A program may use at most 128 MiB of HBM per device.

```python
import math
import jax
import jax.numpy as jnp
from jax import lax

BS = 128
NB = 192
PAIRS = 12
RHS = 8
NC = 24576
BLK_DEV = 24
NR = 512
N_CHAN = 8


def level_of(own_key, dims, pieces, low, top_value):
    def one(position, shards_of):
        steps = jax.random.uniform(jax.random.fold_in(jax.random.fold_in(own_key, 6), position), (shards_of,), jnp.float32, low / len(pieces), top_value / len(pieces))
        return jnp.repeat(jnp.exp(steps), dims[position] // shards_of).reshape((-1,) + (1,) * (len(dims) - position - 1))

    gain = one(*pieces[0])
    for cut in pieces[1:]:
        gain = gain * one(*cut)
    return gain


def different_ones(stream_key, rows, amount, top, lift):
    order = jax.random.permutation(jax.random.fold_in(stream_key, 1), amount)
    pull = order
    for power in range(3):
        pull = pull * pull // amount
    pull = pull * lift // amount
    tickets = jax.random.randint(jax.random.fold_in(stream_key, 2), (rows, amount), 0, 4096) + pull
    holders = jax.random.permutation(jax.random.fold_in(stream_key, 3), rows)[jnp.arange(amount) % rows]
    tickets = jnp.where(jnp.arange(rows)[:, None] == holders[None, :], 1 << 14, tickets)
    priority = tickets * amount + jnp.arange(amount)
    return lax.top_k(priority.astype(jnp.int32), top)[1].astype(jnp.int32)


def normal_values(rng, extent, deviation, most, split=(), kind=jnp.bfloat16):
    level = level_of(rng, extent, split, -0.22, 0.18) if split else 1.0
    entries = jax.random.normal(rng, extent, jnp.float32) * deviation * level
    return jnp.minimum(jnp.maximum(entries, -most), most).astype(kind)


def setup_inputs(seed: int = 0) -> dict:
    seeds = jax.random.split(jax.random.key(seed), 9)
    iterate = normal_values(seeds[0], (NC, NR * RHS), 1.0, 6.0, ((0, 8), (1, 32)))
    source = normal_values(seeds[1], (NC, NR * RHS), 1.0, 6.0, ((0, 8), (1, 32)))
    coupling = normal_values(seeds[2], (NB, PAIRS, BS, BS), (PAIRS * BS) ** -0.5, 0.15625, ((0, 8),))
    pair_rows = different_ones(seeds[3], NB, NB, PAIRS, 0)
    diag_pot = jnp.clip(jax.random.uniform(seeds[4], (NC, NR), jnp.float32, -2.0, 2.0) * level_of(seeds[4], (NC, NR), ((0, 8), (1, 32)), -0.4, 0.0), -2.0, 2.0)
    profile = jnp.clip(jnp.exp(math.log(3.0) - 2.3025851 * jax.random.uniform(seeds[5], (NR,), jnp.float32) ** level_of(seeds[5], (NR,), ((0, 32),), -0.2, 0.2)), 0.3, 3.0)
    regular = normal_values(seeds[6], (NC, NR), 1.0, 6.0, ((0, 8), (1, 32)), jnp.float32)
    irregular = normal_values(seeds[7], (NC, NR), 1.0, 6.0, ((0, 8), (1, 32)), jnp.float32)
    return dict(iterate=iterate, source=source, coupling=coupling, pair_rows=pair_rows, diag_pot=diag_pot, profile=profile, regular=regular, irregular=irregular)


def group_partial(member, iterate_blocks, coupling, pair_rows):
    first_block = member * BLK_DEV
    empty_sum = jnp.zeros((NB, BS, NR * RHS), jnp.float32)

    def add_column(partial_value, offset):
        column = (first_block + offset).astype(jnp.int32)
        block_set = lax.dynamic_index_in_dim(coupling, column, 0, keepdims=False).astype(jnp.float32)
        rows_in = lax.dynamic_index_in_dim(iterate_blocks, column, 0, keepdims=False).astype(jnp.float32)
        product = jnp.einsum('pab,br->par', block_set, rows_in)
        targets = lax.dynamic_index_in_dim(pair_rows, column, 0, keepdims=False).astype(jnp.int32)
        return (partial_value.at[targets].add(product), None)
    partial_value, ignored = lax.scan(add_column, empty_sum, jnp.arange(BLK_DEV, dtype=jnp.int32))
    return partial_value

def reference(iterate, source, coupling, pair_rows, diag_pot, profile, regular, irregular):
    iterate_blocks = iterate.reshape(NB, BS, NR * RHS)
    coupled = jnp.zeros((NB, BS, NR * RHS), jnp.float32)
    for member in range(N_CHAN):
        coupled = coupled + group_partial(member, iterate_blocks, coupling, pair_rows)
    coupled = coupled.reshape(NC, NR, RHS)
    current = iterate.astype(jnp.float32).reshape(NC, NR, RHS)
    driving = diag_pot[:, :, None] * current + profile[None, :, None] * coupled
    quad_step = 1.0 / math.sqrt(NR)
    outward_terms = regular[:, :, None] * driving * quad_step
    inward_terms = irregular[:, :, None] * driving * quad_step
    outward = jnp.cumsum(outward_terms, axis=1)
    inward = jnp.flip(jnp.cumsum(jnp.flip(inward_terms, 1), axis=1), 1) - inward_terms
    updated = source.astype(jnp.float32).reshape(NC, NR, RHS) + irregular[:, :, None] * outward + regular[:, :, None] * inward
    return updated.reshape(NC, NR * RHS).astype(jnp.bfloat16)
```

```python
import math

import jax
import jax.numpy as jnp
from jax import lax
from jax.experimental import pallas as pl
from jax.experimental.pallas import tpu as pltpu
from jax.sharding import PartitionSpec as P

Y, ZL, CORES, ZH, X = 4, 4, 2, 2, 4
PLANE = ZL * CORES
BS = 128
BLOCKS = 24
PAIRS = 12
ROW_BLOCKS = 192
POINTS = 16
SIDES = 8
STEPS = 12
HALF = 6
ZERO_BLOCK = BLOCKS * PAIRS
HIGH = lax.Precision.HIGHEST
MESH = pl.DeviceIdType.MESH
F32 = jnp.float32


def dot0(a, b):
    return lax.dot_general(a, b, (((0,), (0,)), ((), ())), precision=HIGH, preferred_element_type=F32)


def dot1(a, b):
    return lax.dot_general(a, b, (((1,), (1,)), ((), ())), precision=HIGH, preferred_element_type=F32)


def iota(shape, dim):
    return lax.broadcasted_iota(jnp.int32, shape, dim)


def sweep(
    table, coup_hbm, iter_hbm, src_hbm, diag_hbm, prof, reg_hbm, irr_hbm, out,
    coup, itv, src, diag, reg, irr,
    part, rl_p, rl_m, own_p, own_m, cb_p, cb_m, z_out, z_in,
    drv0, reg_e, irr_e, out_l, in_l, p1, p2,
    in_sem, x_send, x_recv, z_send, z_recv, p1_send, p1_recv, p2_send, p2_recv,
):
    slab = lax.axis_index("slab")
    chan = lax.axis_index("chan")
    y = slab // PLANE
    spot = slab % PLANE
    zh = chan // X
    x = chan % X
    x_next, x_last, x_over = (x + 1) % X, (x + 3) % X, (x + 2) % X
    to_next = {"chan": zh * X + x_next}
    to_last = {"chan": zh * X + x_last}
    to_z = {"chan": (1 - zh) * X + x}

    loads = [
        pltpu.make_async_copy(coup_hbm, coup.at[pl.ds(0, ZERO_BLOCK)], in_sem.at[0]),
        pltpu.make_async_copy(iter_hbm, itv, in_sem.at[1]),
        pltpu.make_async_copy(diag_hbm, diag, in_sem.at[2]),
        pltpu.make_async_copy(reg_hbm, reg, in_sem.at[3]),
        pltpu.make_async_copy(irr_hbm, irr, in_sem.at[4]),
        pltpu.make_async_copy(src_hbm, src, in_sem.at[5]),
    ]
    for load in loads:
        load.start()
    coup[ZERO_BLOCK] = jnp.zeros((BS, BS), jnp.bfloat16)

    barrier = pltpu.get_barrier_semaphore()
    for peer in (to_next, to_last, to_z):
        pl.semaphore_signal(barrier, inc=1, device_id=peer, device_id_type=MESH)
    for hop in range(1, PLANE):
        peer = {"slab": y * PLANE + (spot + hop) % PLANE}
        pl.semaphore_signal(barrier, inc=1, device_id=peer, device_id_type=MESH)
    for hop in range(1, Y):
        peer = {"slab": ((y + hop) % Y) * PLANE + spot}
        pl.semaphore_signal(barrier, inc=1, device_id=peer, device_id_type=MESH)

    def dest(step, x_of):
        z_of = jnp.where(step < HALF, 1 - zh, zh)
        return (z_of * X + x_of) * BLOCKS

    def lower(step, x_of):
        return dest(step, x_of) + 2 * (step % HALF)

    def upper(step, x_of):
        return lower(step, x_of) + BLOCKS // 2

    def remote(src_ref, dst_ref, send, recv, peer):
        return pltpu.make_async_remote_copy(
            src_ref=src_ref, dst_ref=dst_ref, send_sem=send, recv_sem=recv,
            device_id=peer, device_id_type=MESH,
        )

    def x_copy(kind, step):
        src_row, landing, peer = (
            (lower(step, x_over), rl_p, to_next),
            (upper(step, x_over), rl_m, to_last),
            (upper(step, x_next), own_p, to_next),
            (lower(step, x_last), own_m, to_last),
            (lower(step, x_next), cb_p, to_next),
            (upper(step, x_last), cb_m, to_last),
        )[kind]
        return remote(
            part.at[pl.ds(src_row, 2)], landing.at[step],
            x_send.at[kind, step], x_recv.at[kind, step], peer,
        )

    def z_copy(piece):
        return remote(z_out.at[piece], z_in.at[piece], z_send.at[piece], z_recv.at[piece], to_z)

    def p1_copy(piece, hop):
        peer = {"slab": y * PLANE + (spot + hop) % PLANE}
        return remote(
            p1.at[piece, spot], p1.at[piece, spot],
            p1_send.at[piece, hop], p1_recv.at[piece, spot], peer,
        )

    def p1_arrival(piece, hop):
        whose = (spot + hop) % PLANE
        peer = {"slab": y * PLANE + whose}
        return remote(
            p1.at[piece, whose], p1.at[piece, whose],
            p1_send.at[piece, hop], p1_recv.at[piece, whose], peer,
        )

    def p2_copy(piece, hop):
        peer = {"slab": ((y + hop) % Y) * PLANE + spot}
        return remote(
            p2.at[piece, y], p2.at[piece, y],
            p2_send.at[piece, hop], p2_recv.at[piece, y], peer,
        )

    def p2_arrival(piece, hop):
        whose = (y + hop) % Y
        peer = {"slab": whose * PLANE + spot}
        return remote(
            p2.at[piece, whose], p2.at[piece, whose],
            p2_send.at[piece, hop], p2_recv.at[piece, whose], peer,
        )

    def multiply(row_a, row_b):
        rows = (row_a, row_a + 1, row_b, row_b + 1)
        total = jnp.zeros((4 * BS, BS), F32)
        for pair in range(BLOCKS // 2):
            left = jnp.concatenate(
                [
                    jnp.concatenate(
                        [coup[table[(2 * pair + k) * ROW_BLOCKS + row]] for k in range(2)], axis=1
                    )
                    for row in rows
                ],
                axis=0,
            )
            right = itv[pl.ds(pair * 2 * BS, 2 * BS), :]
            total = total + jnp.dot(left, right, preferred_element_type=F32)
        part[pl.ds(row_a, 2)] = total[: 2 * BS].reshape(2, BS, BS)
        part[pl.ds(row_b, 2)] = total[2 * BS :].reshape(2, BS, BS)

    spread = (iota((POINTS, BS), 1) // SIDES == iota((POINTS, BS), 0)).astype(F32)
    sides = (iota((SIDES, BS), 1) % SIDES == iota((SIDES, BS), 0)).astype(F32)
    from_n, to_n = iota((BS, BS), 0), iota((BS, BS), 1)
    same_side = from_n % SIDES == to_n % SIDES
    upto = (same_side & (from_n // SIDES <= to_n // SIDES)).astype(F32)
    above = (same_side & (from_n // SIDES > to_n // SIDES)).astype(F32)
    prof_e = dot0(prof[...], spread)
    quad_step = 1.0 / math.sqrt(POINTS * Y * PLANE)

    def columns(piece, half):
        return pl.ds(pl.multiple_of(piece * 2 * BS + half * (BLOCKS // 2) * BS, 2 * BS), 2 * BS)

    def blocks(piece, half):
        return pl.ds(2 * piece + half * (BLOCKS // 2), 2)

    def expand(piece):
        for half in range(2):
            cols, rows = columns(piece, half), blocks(piece, half)
            shape = (2, BS, BS)
            reg_e[rows] = dot0(reg[:, cols], spread).reshape(shape)
            irr_e[rows] = dot0(irr[:, cols], spread).reshape(shape)
            now = itv[cols, :].astype(F32)
            drv0[rows] = (dot0(diag[:, cols], spread) * now).reshape(shape)

    def combine(step):
        for kind, landing in ((0, rl_p), (1, rl_m)):
            x_copy(kind, step).wait_recv()
        lo, hi = pl.ds(lower(step, x_next), 2), pl.ds(upper(step, x_last), 2)
        part[lo] = part[lo] + rl_p[step]
        x_copy(4, step).start()
        part[hi] = part[hi] + rl_m[step]
        x_copy(5, step).start()

    def sums(step):
        for kind in (2, 3, 4, 5):
            x_copy(kind, step).wait_recv()
        lo = part[pl.ds(lower(step, x), 2)] + cb_p[step] + own_m[step]
        hi = part[pl.ds(upper(step, x), 2)] + own_p[step] + cb_m[step]
        return lo, hi

    def finish_far(step):
        lo, hi = sums(step)
        z_out[step, pl.ds(0, 2)] = lo
        z_out[step, pl.ds(2, 2)] = hi
        z_copy(step).start()

    def finish_near(step):
        piece = step - HALF
        z_copy(piece).wait_recv()
        both = sums(step)
        for half in range(2):
            rows = blocks(piece, half)
            coupled = both[half] + z_in[piece, pl.ds(2 * half, 2)]
            driving = (drv0[rows] + prof_e * coupled) * quad_step
            outs = (reg_e[rows] * driving).reshape(2 * BS, BS)
            ins = (irr_e[rows] * driving).reshape(2 * BS, BS)
            cols = pl.ds(half * 2 * BS, 2 * BS)
            p1[piece, spot, pl.ds(0, SIDES), cols] = dot1(sides, outs)
            p1[piece, spot, pl.ds(SIDES, SIDES), cols] = dot1(sides, ins)
            out_l[rows] = jnp.dot(outs, upto, precision=HIGH, preferred_element_type=F32).reshape(2, BS, BS)
            in_l[rows] = jnp.dot(ins, above, precision=HIGH, preferred_element_type=F32).reshape(2, BS, BS)
        for hop in range(1, PLANE):
            p1_copy(piece, hop).start()

    def plane_sum(piece):
        for hop in range(1, PLANE):
            p1_arrival(piece, hop).wait_recv()
        total = p1[piece, 0]
        for whose in range(1, PLANE):
            total = total + p1[piece, whose]
        p2[piece, y] = total
        for hop in range(1, Y):
            p2_copy(piece, hop).start()

    def emit(piece):
        for hop in range(1, Y):
            p2_arrival(piece, hop).wait_recv()
        before = jnp.zeros((SIDES, 4 * BS), F32)
        after = jnp.zeros((SIDES, 4 * BS), F32)
        for whose in range(PLANE):
            before = before + jnp.where(whose < spot, p1[piece, whose, pl.ds(0, SIDES)], 0.0)
            after = after + jnp.where(whose > spot, p1[piece, whose, pl.ds(SIDES, SIDES)], 0.0)
        for whose in range(Y):
            before = before + jnp.where(whose < y, p2[piece, whose, pl.ds(0, SIDES)], 0.0)
            after = after + jnp.where(whose > y, p2[piece, whose, pl.ds(SIDES, SIDES)], 0.0)
        for half in range(2):
            rows = blocks(piece, half)
            take = slice(half * 2 * BS, (half + 1) * 2 * BS)
            outward = out_l[rows] + dot0(before[:, take], sides).reshape(2, BS, BS)
            inward = in_l[rows] + dot0(after[:, take], sides).reshape(2, BS, BS)
            updated = src[rows].astype(F32) + irr_e[rows] * outward + reg_e[rows] * inward
            out[rows] = updated.astype(jnp.bfloat16)

    loads[0].wait()
    loads[1].wait()
    pl.semaphore_wait(barrier, 3 + (PLANE - 1) + (Y - 1))

    def one_step(step, _):
        @pl.when(step < STEPS)
        def _():
            multiply(lower(step, x_over), upper(step, x_over))
            x_copy(0, step).start()
            x_copy(1, step).start()

        @pl.when((step >= 1) & (step <= STEPS))
        def _():
            combine(step - 1)

        @pl.when(step < STEPS)
        def _():
            multiply(upper(step, x_next), lower(step, x_last))
            x_copy(2, step).start()
            x_copy(3, step).start()

        @pl.when((step >= 2) & (step < HALF + 2))
        def _():
            finish_far(step - 2)

        @pl.when(step >= HALF + 2)
        def _():
            @pl.when(step < STEPS + 2)
            def _():
                finish_near(step - 2)

        @pl.when(step < STEPS)
        def _():
            multiply(lower(step, x_next), upper(step, x_last))
            multiply(lower(step, x), upper(step, x))

        @pl.when(step == 0)
        def _():
            for load in loads[2:]:
                load.wait()

        @pl.when(step < HALF)
        def _():
            expand(step)

        @pl.when((step >= HALF + 3) & (step < STEPS + 3))
        def _():
            plane_sum(step - HALF - 3)

        @pl.when(step >= HALF + 4)
        def _():
            emit(step - HALF - 4)

        return 0

    lax.fori_loop(0, STEPS + 4, one_step, 0)

    def drain(step, _):
        for kind in range(6):
            x_copy(kind, step).wait_send()
        return 0

    lax.fori_loop(0, STEPS, drain, 0)

    def drain_pieces(piece, _):
        z_copy(piece).wait_send()
        for hop in range(1, PLANE):
            p1_copy(piece, hop).wait_send()
        for hop in range(1, Y):
            p2_copy(piece, hop).wait_send()
        return 0

    lax.fori_loop(0, HALF, drain_pieces, 0)


def per_device(iterate, source, coupling, pair_rows, diag_pot, profile, regular, irregular):
    channels = iterate.shape[0]
    pair_index = jnp.arange(BLOCKS * PAIRS, dtype=jnp.int32).reshape(BLOCKS, PAIRS, 1)
    named = pair_rows[:, :, None] == jnp.arange(ROW_BLOCKS, dtype=jnp.int32)
    table = ZERO_BLOCK + jnp.sum(jnp.where(named, pair_index - ZERO_BLOCK, 0), axis=1)
    anywhere = pl.BlockSpec(memory_space=pl.ANY)
    vmem = pl.BlockSpec(memory_space=pltpu.VMEM)
    blocked = (BLOCKS, BS, BS)
    landing = pltpu.VMEM((STEPS, 2, BS, BS), F32)
    dma = pltpu.SemaphoreType.DMA
    out = pl.pallas_call(
        sweep,
        out_shape=jax.ShapeDtypeStruct(blocked, jnp.bfloat16),
        in_specs=[pl.BlockSpec(memory_space=pltpu.SMEM)] + [anywhere] * 4 + [vmem] + [anywhere] * 2,
        out_specs=vmem,
        scratch_shapes=[
            pltpu.VMEM((ZERO_BLOCK + 1, BS, BS), jnp.bfloat16),
            pltpu.VMEM((channels, BS), jnp.bfloat16),
            pltpu.VMEM(blocked, jnp.bfloat16),
            pltpu.VMEM((POINTS, channels), F32),
            pltpu.VMEM((POINTS, channels), F32),
            pltpu.VMEM((POINTS, channels), F32),
            pltpu.VMEM((ROW_BLOCKS, BS, BS), F32),
            landing, landing, landing, landing, landing, landing,
            pltpu.VMEM((HALF, 4, BS, BS), F32),
            pltpu.VMEM((HALF, 4, BS, BS), F32),
            pltpu.VMEM(blocked, F32),
            pltpu.VMEM(blocked, F32),
            pltpu.VMEM(blocked, F32),
            pltpu.VMEM(blocked, F32),
            pltpu.VMEM(blocked, F32),
            pltpu.VMEM((HALF, PLANE, 2 * SIDES, 4 * BS), F32),
            pltpu.VMEM((HALF, Y, 2 * SIDES, 4 * BS), F32),
            dma((6,)),
            dma((6, STEPS)), dma((6, STEPS)),
            dma((HALF,)), dma((HALF,)),
            dma((HALF, PLANE)), dma((HALF, PLANE)),
            dma((HALF, Y)), dma((HALF, Y)),
        ],
        compiler_params=pltpu.CompilerParams(
            collective_id=0, has_side_effects=True, vmem_limit_bytes=60 * 2**20
        ),
        name="sweep",
    )(
        table.reshape(-1),
        coupling.reshape(BLOCKS * PAIRS, BS, BS),
        iterate,
        source.reshape(blocked),
        diag_pot.T,
        profile.reshape(POINTS, 1),
        regular.T,
        irregular.T,
    )
    return out.reshape(channels, BS)


def solution(mesh):
    placed = (
        P("chan", "slab"),
        P("chan", "slab"),
        P("chan", None, None, None),
        P("chan", None),
        P("chan", "slab"),
        P("slab"),
        P("chan", "slab"),
        P("chan", "slab"),
    )
    return jax.shard_map(
        per_device, mesh=mesh, in_specs=placed, out_specs=P("chan", "slab"), check_vma=False
    )
```

```python
import math

import jax
import jax.numpy as jnp
from jax import lax
from jax.experimental import pallas as pl
from jax.experimental.pallas import tpu as pltpu
from jax.sharding import PartitionSpec as P

Y, ZL, CORES, ZH, X = 4, 4, 2, 2, 4
PLANE = ZL * CORES
BS = 128
BLOCKS = 24
PAIRS = 12
ROW_BLOCKS = 192
POINTS = 16
SIDES = 8
CHANNELS = BLOCKS * BS
HALF_ROWS = CHANNELS // 2
STEPS = 12
HALF = 6
PIECE = 256
TAIL = ((1280, 128), (1408, 64), (1472, 64))
SENDS = STEPS - 1 + len(TAIL)
LOADS = 4
SHARE = BLOCKS * PAIRS // LOADS
HIGH = lax.Precision.HIGHEST
MESH = pl.DeviceIdType.MESH
F32 = jnp.float32


def dot0(a, b):
    return lax.dot_general(a, b, (((0,), (0,)), ((), ())), precision=HIGH, preferred_element_type=F32)


def dot1(a, b):
    return lax.dot_general(a, b, (((1,), (1,)), ((), ())), precision=HIGH, preferred_element_type=F32)


def iota(shape, dim):
    return lax.broadcasted_iota(jnp.int32, shape, dim)


def sweep(
    pairs, coup_hbm, iter_hbm, src_hbm, diag_hbm, prof_hbm, reg_hbm, irr_hbm, out_hbm,
    square, prof, table_v, table, coup_0, coup_1, coup_2, coup_3, itv, src, diag, reg, irr, out,
    part, relayed, arrived, z_out, z_in,
    drv0, reg_e, irr_e, local, own_0, own_1, own_2, near_0, near_1, near_2,
    in_sem, out_sem, x_send, x_recv, z_send, z_recv,
    scan_send, scan_recv,
):
    slab = lax.axis_index("slab")
    chan = lax.axis_index("chan")
    y = slab // PLANE
    spot = slab % PLANE
    zl, core = spot // CORES, spot % CORES
    zh = chan // X
    x = chan % X
    x_next, x_last, x_over = (x + 1) % X, (x + 3) % X, (x + 2) % X
    to_next = {"chan": zh * X + x_next}
    to_last = {"chan": zh * X + x_last}
    to_z = {"chan": (1 - zh) * X + x}
    near_core = [{"slab": slab + 1 - 2 * core}]
    near_z = [{"slab": y * PLANE + (zl + hop) % ZL * CORES + core} for hop in range(1, ZL)]
    near_y = [{"slab": (y + hop) % Y * PLANE + spot} for hop in range(1, Y)]

    coups = (coup_0, coup_1, coup_2, coup_3)
    loads = [
        pltpu.make_async_copy(
            coup_hbm.at[pl.ds(i * SHARE, SHARE)], coups[i].at[pl.ds(0, SHARE)], in_sem.at[i]
        )
        for i in range(LOADS)
    ] + [
        pltpu.make_async_copy(given, held, in_sem.at[LOADS + i])
        for i, (given, held) in enumerate(
            ((iter_hbm, itv), (diag_hbm, diag), (reg_hbm, reg), (irr_hbm, irr), (src_hbm, src))
        )
    ]
    prof_load = pltpu.make_async_copy(prof_hbm, prof, in_sem.at[LOADS + 6])
    first_loads, later_loads = loads[: LOADS + 1], loads[LOADS + 1 :] + [prof_load]
    loads[LOADS].start()
    for load in loads[:LOADS]:
        load.start()

    barrier = pltpu.get_barrier_semaphore()
    for peer in (to_next, to_last, to_z):
        pl.semaphore_signal(barrier, inc=1, device_id=peer, device_id_type=MESH)
    for peer in near_core + near_z + near_y:
        pl.semaphore_signal(barrier, inc=1, device_id=peer, device_id_type=MESH)

    shape = (BLOCKS, 2 * BS)
    found = jnp.full(shape, SHARE, jnp.int32)
    square[:PAIRS, :BLOCKS] = pairs[...]
    named = square[...].T
    for p in range(PAIRS):
        found = jnp.where(named[:BLOCKS, p : p + 1] == iota(shape, 1), iota(shape, 0) % (SHARE // PAIRS) * PAIRS + p, found)
    table_v[...] = found
    to_scalars = pltpu.make_async_copy(table_v, table, in_sem.at[LOADS + 5])
    to_scalars.start()
    for coup in coups:
        coup[SHARE] = jnp.zeros((BS, BS), jnp.bfloat16)

    def aligned(row):
        return pl.multiple_of(row, 64)

    def dest(step, x_of):
        z_of = jnp.where(step < HALF, 1 - zh, zh)
        return (z_of * X + x_of) * CHANNELS

    def lower(step, at, x_of):
        return aligned(dest(step, x_of) + at)

    def upper(step, at, x_of):
        return aligned(dest(step, x_of) + at + HALF_ROWS)

    def landed(step, at):
        return jnp.where(step < HALF, 0, HALF_ROWS) + at

    def remote(src_ref, dst_ref, send, recv, peer):
        return pltpu.make_async_remote_copy(
            src_ref=src_ref, dst_ref=dst_ref, send_sem=send, recv_sem=recv,
            device_id=peer, device_id_type=MESH,
        )

    def x_copy(kind, step, at, rows):
        src_row, peer = (
            (lower(step, at, x_over), to_next),
            (upper(step, at, x_over), to_last),
            (upper(step, at, x_next), to_next),
            (lower(step, at, x_last), to_last),
            (lower(step, at, x_next), to_next),
            (upper(step, at, x_last), to_last),
        )[kind]
        if kind < 2:
            landing, first = relayed, 2 * landed(step, at) + kind * rows
        else:
            landing, first = arrived, 4 * landed(step, at) + (kind - 2) * rows
        return remote(
            part.at[pl.ds(src_row, rows)], landing.at[pl.ds(aligned(first), rows)],
            x_send.at[kind], x_recv.at[0 if kind < 2 else 1, step], peer,
        )

    def x_start(kinds, step, at, rows):
        for kind in kinds:
            x_copy(kind, step, at, rows).start()

    def x_wait(place, step, at, rows):
        landing, count = ((relayed, 2), (arrived, 4))[place]
        whole = landing.at[pl.ds(aligned(count * landed(step, at)), count * rows)]
        remote(whole, whole, x_send.at[0], x_recv.at[place, step], to_next).wait_recv()

    def z_copy(step):
        rows = pl.ds(aligned(step * 2 * PIECE), 2 * PIECE)
        return remote(z_out.at[rows], z_in.at[rows], z_send.at[0], z_recv.at[step], to_z)

    levels = (
        (CORES, core, own_0, near_0, near_core),
        (ZL, zl, own_1, near_1, near_z),
        (Y, y, own_2, near_2, near_y),
    )

    def spans(at, rows):
        return pl.ds(at * 2 // BS, rows * 2 // BS)

    def scan_start(level, slot, at, rows):
        _, _, own, near, peers = levels[level]
        here = spans(at, rows)
        for i, peer in enumerate(peers):
            remote(
                own.at[here], near.at[i, here], scan_send.at[level], scan_recv.at[level, slot], peer
            ).start()

    def scan_wait(level, slot, at, rows):
        _, _, _, near, peers = levels[level]
        whole = near.at[:, spans(at, rows)]
        remote(whole, whole, scan_send.at[level], scan_recv.at[level, slot], peers[0]).wait_recv()

    def scan_total(level, here):
        size, _, own, near, _ = levels[level]
        return sum((near[i, here] for i in range(size - 1)), own[here])

    def scan_part(level, here, lanes, later):
        size, mine, _, near, _ = levels[level]
        terms = []
        for i in range(size - 1):
            whose = (mine + size - 1 - i) % size
            counts = whose > mine if later else whose < mine
            terms.append(jnp.where(counts, near[i, here, lanes, :], 0.0))
        return sum(terms[1:], terms[0])

    def out_copy(at, rows, half):
        here = pl.ds(aligned(at + half * HALF_ROWS), rows)
        return pltpu.make_async_copy(out.at[here], out_hbm.at[here], out_sem.at[0])

    def place(step):
        return lax.rem(step, HALF) * PIECE

    def multiply(step, group, ready=None):
        x_a = (x + jnp.where(group == 0, 2, jnp.where(group == 3, 0, 1))) % X
        x_b = (x + jnp.where(group == 0, 2, jnp.where(group == 3, 0, 3))) % X
        cross = group == 1
        at = place(step)
        row_a = aligned(dest(step, x_a) + at + jnp.where(cross, HALF_ROWS, 0))
        row_b = aligned(dest(step, x_b) + at + jnp.where(cross, 0, HALF_ROWS))
        block_a, block_b = row_a // BS, row_b // BS
        blocks = (block_a, block_a + 1, block_b, block_b + 1)
        total = jnp.zeros((2 * PIECE, BS), F32)
        for pair in range(BLOCKS // 2):
            if ready is not None:
                ready(pair)
            coup = coups[2 * pair * PAIRS // SHARE]
            left = jnp.concatenate(
                [
                    jnp.concatenate([coup[table[2 * pair + k, block]] for k in range(2)], axis=1)
                    for block in blocks
                ],
                axis=0,
            )
            right = itv[pl.ds(pair * 2 * BS, 2 * BS), :]
            total = total + jnp.dot(left, right, preferred_element_type=F32)
        part[pl.ds(row_a, PIECE)] = total[:PIECE]
        part[pl.ds(row_b, PIECE)] = total[PIECE:]

    spread = (iota((POINTS, BS), 1) // SIDES == iota((POINTS, BS), 0)).astype(F32)
    sides = (iota((SIDES, BS), 1) % SIDES == iota((SIDES, BS), 0)).astype(F32)
    from_n, to_n = iota((BS, BS), 0), iota((BS, BS), 1)
    same_side = from_n % SIDES == to_n % SIDES
    upto = (same_side & (from_n // SIDES <= to_n // SIDES)).astype(F32)
    above = (same_side & (from_n // SIDES > to_n // SIDES)).astype(F32)

    def profile_row():
        return jnp.dot(prof[...], spread, precision=HIGH, preferred_element_type=F32)

    quad_step = 1.0 / math.sqrt(POINTS * Y * PLANE)

    def both(ref, at, rows):
        return jnp.concatenate(
            [ref[pl.ds(aligned(at), rows), :], ref[pl.ds(aligned(at + HALF_ROWS), rows), :]], axis=0
        )

    def expand(step):
        for half in range(2):
            here = pl.ds(pl.multiple_of(step * PIECE + half * HALF_ROWS, PIECE), PIECE)
            reg_e[here] = dot0(reg[:, here], spread)
            irr_e[here] = dot0(irr[:, here], spread)
            drv0[here] = dot0(diag[:, here], spread) * itv[here, :].astype(F32)

    def combine(step, at, rows):
        x_wait(0, step, at, rows)
        lo, hi = pl.ds(lower(step, at, x_next), rows), pl.ds(upper(step, at, x_last), rows)
        base = 2 * landed(step, at)
        part[lo] = part[lo] + relayed[pl.ds(aligned(base), rows)]
        x_start((4,), step, at, rows)
        part[hi] = part[hi] + relayed[pl.ds(aligned(base + rows), rows)]
        x_start((5,), step, at, rows)

    def own_sums(step, at, rows):
        x_wait(1, step, at, rows)
        base = 4 * landed(step, at)
        up_own, lo_own, lo_sum, up_sum = [
            arrived[pl.ds(aligned(base + i * rows), rows)] for i in range(4)
        ]
        lo = part[pl.ds(lower(step, at, x), rows)] + lo_own + lo_sum
        hi = part[pl.ds(upper(step, at, x), rows)] + up_own + up_sum
        return lo, hi

    def finish_far(step):
        lo, hi = own_sums(step, step * PIECE, PIECE)
        z_out[pl.ds(aligned(step * 2 * PIECE), PIECE)] = lo
        z_out[pl.ds(aligned(step * 2 * PIECE + PIECE), PIECE)] = hi
        z_copy(step).start()

    def finish_near(step, slot, at, rows, crossed):
        if crossed is not None:
            z_copy(crossed).wait_recv()
        lo, hi = own_sums(step, at, rows)
        base = at // PIECE * PIECE + at
        lo = lo + z_in[pl.ds(aligned(base), rows)]
        hi = hi + z_in[pl.ds(aligned(base + PIECE), rows)]
        coupled = jnp.concatenate([lo, hi], axis=0)
        driving = (both(drv0, at, rows) + profile_row() * coupled) * quad_step
        regular, irregular = both(reg_e, at, rows), both(irr_e, at, rows)
        outs, ins = regular * driving, irregular * driving
        totals = jnp.concatenate([dot1(sides, outs), dot1(sides, ins)], axis=0)
        for i in range(2 * rows // BS):
            own_0[at * 2 // BS + i] = totals[:, i * BS : (i + 1) * BS]
        scan_start(0, slot, at, rows)
        outward = jnp.dot(outs, upto, precision=HIGH, preferred_element_type=F32)
        inward = jnp.dot(ins, above, precision=HIGH, preferred_element_type=F32)
        result = both(src, at, rows).astype(F32) + irregular * outward + regular * inward
        local[pl.ds(aligned(at), rows)] = result[:rows]
        local[pl.ds(aligned(at + HALF_ROWS), rows)] = result[rows:]

    def chip_sum(slot, at, rows):
        scan_wait(0, slot, at, rows)
        own_1[spans(at, rows)] = scan_total(0, spans(at, rows))
        scan_start(1, slot, at, rows)

    def plane_sum(slot, at, rows):
        scan_wait(1, slot, at, rows)
        own_2[spans(at, rows)] = scan_total(1, spans(at, rows))
        scan_start(2, slot, at, rows)

    def emit(slot, at, rows):
        here = spans(at, rows)
        count = 2 * rows // BS

        sides_of = ((pl.ds(0, SIDES), False), (pl.ds(SIDES, SIDES), True))
        carries = [
            scan_part(0, here, lanes, later) + scan_part(1, here, lanes, later)
            for lanes, later in sides_of
        ]
        scan_wait(2, slot, at, rows)
        outward, inward = [
            jnp.concatenate([total[i] for i in range(count)], axis=1)
            for total in (
                carry + scan_part(2, here, lanes, later)
                for carry, (lanes, later) in zip(carries, sides_of)
            )
        ]
        updated = both(local, at, rows)
        updated = updated + both(irr_e, at, rows) * dot0(outward, sides)
        updated = updated + both(reg_e, at, rows) * dot0(inward, sides)
        updated = updated.astype(jnp.bfloat16)
        for half in range(2):
            out[pl.ds(aligned(at + half * HALF_ROWS), rows), :] = updated[half * rows : (half + 1) * rows]
            out_copy(at, rows, half).start()

    def regular_piece(call, piece):
        call(piece, piece * PIECE, PIECE)

    to_scalars.wait()
    loads[LOADS].wait()

    def ready(pair):
        if pair % (BLOCKS // 2 // LOADS) == 0:
            loads[pair // (BLOCKS // 2 // LOADS)].wait()

    multiply(0, 0, ready)
    for load in later_loads:
        load.start()
    pl.semaphore_wait(barrier, 3 + 1 + (ZL - 1) + (Y - 1))
    x_start((0, 1), 0, 0, PIECE)
    multiply(0, 1)
    x_start((2, 3), 0, 0, PIECE)

    def multiply_more(step, first):
        def one_group(group, _):
            multiply(step, group)
            return 0

        lax.fori_loop(first, 4, one_group, 0)

    multiply_more(0, 2)
    for load in later_loads:
        load.wait()

    def one_step(step, _):
        @pl.when(step >= 1)
        def _():
            at = place(step)
            x_start((0, 1), step, at, PIECE)
            combine(step - 1, place(step - 1), PIECE)
            x_start((2, 3), step, at, PIECE)

        @pl.when((step >= 2) & (step < HALF + 2))
        def _():
            finish_far(step - 2)

        @pl.when(step >= HALF + 2)
        def _():
            piece = step - HALF - 2
            finish_near(step - 2, piece, piece * PIECE, PIECE, piece)

        multiply_more(step + 1, 0)

        @pl.when(step < HALF)
        def _():
            expand(step)

        @pl.when(step >= HALF + 3)
        def _():
            regular_piece(chip_sum, step - HALF - 3)

        @pl.when(step >= HALF + 4)
        def _():
            regular_piece(plane_sum, step - HALF - 4)

        return 0

    lax.fori_loop(0, STEPS - 1, one_step, 0)

    last = STEPS - 1

    def send(kinds, i):
        x_start(kinds, last + i, *TAIL[i])

    def meet(i):
        combine(last + i, *TAIL[i])

    def finish(i):
        finish_near(last + i, HALF - 1 + i, *TAIL[i], HALF - 1 if i == 0 else None)

    def finish_regular(piece):
        finish_near(HALF + piece, piece, piece * PIECE, PIECE, piece)

    def small_piece(call, i):
        call(HALF - 1 + i, *TAIL[i])

    send((0, 1), 0)
    combine(last - 1, (HALF - 2) * PIECE, PIECE)
    send((2, 3), 0)
    send((0, 1), 1)
    send((2, 3), 1)
    send((0, 1), 2)
    finish_regular(3)
    meet(0)
    send((2, 3), 2)
    regular_piece(chip_sum, 2)
    regular_piece(plane_sum, 1)
    regular_piece(emit, 0)
    meet(1)
    meet(2)
    finish_regular(4)
    regular_piece(chip_sum, 3)
    regular_piece(plane_sum, 2)
    finish(0)
    regular_piece(chip_sum, 4)
    small_piece(chip_sum, 0)
    finish(1)
    finish(2)
    regular_piece(plane_sum, 3)
    small_piece(chip_sum, 1)
    small_piece(chip_sum, 2)
    regular_piece(emit, 1)
    regular_piece(plane_sum, 4)
    small_piece(plane_sum, 0)
    small_piece(plane_sum, 1)
    small_piece(plane_sum, 2)
    regular_piece(emit, 2)
    regular_piece(emit, 3)
    regular_piece(emit, 4)
    for i in range(len(TAIL)):
        small_piece(emit, i)

    for kind in range(6):
        whole = part.at[pl.ds(0, CHANNELS)]
        remote(whole, whole, x_send.at[kind], x_recv.at[0, 0], to_next).wait_send()
    remote(z_out, z_in, z_send.at[0], z_recv.at[0], to_z).wait_send()
    for level, (_, _, _, near, peers) in enumerate(levels):
        remote(near, near, scan_send.at[level], scan_recv.at[level, 0], peers[0]).wait_send()
    pltpu.make_async_copy(out, out_hbm, out_sem.at[0]).wait()


def per_device(iterate, source, coupling, pair_rows, diag_pot, profile, regular, irregular):
    anywhere = pl.BlockSpec(memory_space=pl.ANY)
    wide = pltpu.VMEM((CHANNELS, BS), F32)
    whole = pltpu.VMEM((CHANNELS, BS), jnp.bfloat16)
    narrow = pltpu.VMEM((POINTS, CHANNELS), F32)
    def tiles(*count):
        return pltpu.VMEM((*count, CHANNELS // BS, 2 * SIDES, BS), F32)

    share = pltpu.VMEM((SHARE + 1, BS, BS), jnp.bfloat16)
    dma = pltpu.SemaphoreType.DMA
    result = jax.ShapeDtypeStruct((CHANNELS, BS), jnp.bfloat16)
    updated = pl.pallas_call(
        sweep,
        out_shape=result,
        in_specs=[pl.BlockSpec(memory_space=pltpu.VMEM)] + [anywhere] * 7,
        out_specs=anywhere,
        scratch_shapes=[
            pltpu.VMEM((BS, BS), jnp.int32),
            pltpu.VMEM((1, POINTS), F32),
            pltpu.VMEM((BLOCKS, 2 * BS), jnp.int32),
            pltpu.SMEM((BLOCKS, 2 * BS), jnp.int32),
            share, share, share, share,
            whole, whole, narrow, narrow, narrow, whole,
            pltpu.VMEM((ROW_BLOCKS * BS, BS), F32),
            pltpu.VMEM((2 * CHANNELS, BS), F32),
            pltpu.VMEM((4 * CHANNELS, BS), F32),
            wide, wide, wide, wide, wide, wide,
            tiles(), tiles(), tiles(), tiles(CORES - 1), tiles(ZL - 1), tiles(Y - 1),
            dma((LOADS + 7,)), dma((1,)),
            dma((6,)), dma((2, SENDS)),
            dma((1,)), dma((HALF,)),
            dma((3,)), dma((3, HALF - 1 + len(TAIL))),
        ],
        compiler_params=pltpu.CompilerParams(
            collective_id=0, has_side_effects=True, vmem_limit_bytes=60 * 2**20
        ),
        name="sweep",
    )(
        pair_rows.T,
        coupling.reshape(BLOCKS * PAIRS, BS, BS),
        iterate,
        source,
        diag_pot.T,
        profile.reshape(1, POINTS),
        regular.T,
        irregular.T,
    )
    return updated


def solution(mesh):
    placed = (
        P("chan", "slab"),
        P("chan", "slab"),
        P("chan", None, None, None),
        P("chan", None),
        P("chan", "slab"),
        P("slab"),
        P("chan", "slab"),
        P("chan", "slab"),
    )
    return jax.shard_map(
        per_device, mesh=mesh, in_specs=placed, out_specs=P("chan", "slab"), check_vma=False
    )
```

```python
import math

import jax
import jax.numpy as jnp
from jax import lax
from jax.experimental import pallas as pl
from jax.experimental.pallas import tpu as pltpu
from jax.sharding import PartitionSpec as P

Y, ZL, CORES, ZH, X = 4, 4, 2, 2, 4
PLANE = ZL * CORES
BS = 128
BLOCKS = 24
PAIRS = 12
ROW_BLOCKS = 192
POINTS = 16
SIDES = 8
CHANNELS = BLOCKS * BS
HALF_ROWS = CHANNELS // 2
STEPS = 12
HALF = 6
PIECE = 256
TAIL = ((1280, 128), (1408, 64), (1472, 64))
SENDS = STEPS - 1 + len(TAIL)
LOADS = 4
SHARE = BLOCKS * PAIRS // LOADS
HIGH = lax.Precision.HIGHEST
MESH = pl.DeviceIdType.MESH
F32 = jnp.float32


def dot0(a, b):
    return lax.dot_general(a, b, (((0,), (0,)), ((), ())), precision=HIGH, preferred_element_type=F32)


def dot1(a, b):
    return lax.dot_general(a, b, (((1,), (1,)), ((), ())), precision=HIGH, preferred_element_type=F32)


def iota(shape, dim):
    return lax.broadcasted_iota(jnp.int32, shape, dim)


def sweep(
    pairs, coup_hbm, iter_hbm, src_hbm, diag_hbm, prof_hbm, reg_hbm, irr_hbm, out_hbm,
    square, prof, table_v, table, coup_0, coup_1, coup_2, coup_3, itv, src, diag, reg, irr, out,
    part, relayed, arrived, z_out, z_in,
    drv0, reg_e, irr_e, local, own_0, own_1, own_2, near_0, near_1, near_2,
    in_sem, out_sem, x_send, x_recv, z_send, z_recv,
    scan_send, scan_recv,
):
    slab = lax.axis_index("slab")
    chan = lax.axis_index("chan")
    y = slab // PLANE
    spot = slab % PLANE
    zl, core = spot // CORES, spot % CORES
    zh = chan // X
    x = chan % X
    x_next, x_last, x_over = (x + 1) % X, (x + 3) % X, (x + 2) % X
    to_next = {"chan": zh * X + x_next}
    to_last = {"chan": zh * X + x_last}
    to_z = {"chan": (1 - zh) * X + x}
    near_core = [{"slab": slab + 1 - 2 * core}]
    near_z = [{"slab": y * PLANE + (zl + hop) % ZL * CORES + core} for hop in range(1, ZL)]
    near_y = [{"slab": (y + hop) % Y * PLANE + spot} for hop in range(1, Y)]

    coups = (coup_0, coup_1, coup_2, coup_3)
    loads = [
        pltpu.make_async_copy(
            coup_hbm.at[pl.ds(i * SHARE, SHARE)], coups[i].at[pl.ds(0, SHARE)], in_sem.at[i]
        )
        for i in range(LOADS)
    ] + [
        pltpu.make_async_copy(given, held, in_sem.at[LOADS + i])
        for i, (given, held) in enumerate(
            ((iter_hbm, itv), (diag_hbm, diag), (reg_hbm, reg), (irr_hbm, irr), (src_hbm, src))
        )
    ]
    prof_load = pltpu.make_async_copy(prof_hbm, prof, in_sem.at[LOADS + 6])
    first_loads, later_loads = loads[: LOADS + 1], loads[LOADS + 1 :] + [prof_load]
    loads[LOADS].start()
    for load in loads[:LOADS]:
        load.start()

    barrier = pltpu.get_barrier_semaphore()
    for peer in (to_next, to_last, to_z):
        pl.semaphore_signal(barrier, inc=1, device_id=peer, device_id_type=MESH)
    for peer in near_core + near_z + near_y:
        pl.semaphore_signal(barrier, inc=1, device_id=peer, device_id_type=MESH)

    shape = (BLOCKS, 2 * BS)
    found = jnp.full(shape, SHARE, jnp.int32)
    square[:PAIRS, :BLOCKS] = pairs[...]
    named = square[...].T
    for p in range(PAIRS):
        found = jnp.where(named[:BLOCKS, p : p + 1] == iota(shape, 1), iota(shape, 0) % (SHARE // PAIRS) * PAIRS + p, found)
    table_v[...] = found
    to_scalars = pltpu.make_async_copy(table_v, table, in_sem.at[LOADS + 5])
    to_scalars.start()
    for coup in coups:
        coup[SHARE] = jnp.zeros((BS, BS), jnp.bfloat16)

    def aligned(row):
        return pl.multiple_of(row, 64)

    def dest(step, x_of):
        z_of = jnp.where(step < HALF, 1 - zh, zh)
        return (z_of * X + x_of) * CHANNELS

    def lower(step, at, x_of):
        return aligned(dest(step, x_of) + at)

    def upper(step, at, x_of):
        return aligned(dest(step, x_of) + at + HALF_ROWS)

    def landed(step, at):
        return jnp.where(step < HALF, 0, HALF_ROWS) + at

    def remote(src_ref, dst_ref, send, recv, peer):
        return pltpu.make_async_remote_copy(
            src_ref=src_ref, dst_ref=dst_ref, send_sem=send, recv_sem=recv,
            device_id=peer, device_id_type=MESH,
        )

    def x_copy(kind, step, at, rows):
        src_row, peer = (
            (lower(step, at, x_over), to_next),
            (upper(step, at, x_over), to_last),
            (upper(step, at, x_next), to_next),
            (lower(step, at, x_last), to_last),
            (lower(step, at, x_next), to_next),
            (upper(step, at, x_last), to_last),
        )[kind]
        if kind < 2:
            landing, first = relayed, 2 * landed(step, at) + kind * rows
        else:
            landing, first = arrived, 4 * landed(step, at) + (kind - 2) * rows
        return remote(
            part.at[pl.ds(src_row, rows)], landing.at[pl.ds(aligned(first), rows)],
            x_send.at[kind], x_recv.at[0 if kind < 2 else 1, step], peer,
        )

    def x_start(kinds, step, at, rows):
        for kind in kinds:
            x_copy(kind, step, at, rows).start()

    def x_wait(place, step, at, rows):
        landing, count = ((relayed, 2), (arrived, 4))[place]
        whole = landing.at[pl.ds(aligned(count * landed(step, at)), count * rows)]
        remote(whole, whole, x_send.at[0], x_recv.at[place, step], to_next).wait_recv()

    def z_copy(step):
        rows = pl.ds(aligned(step * 2 * PIECE), 2 * PIECE)
        return remote(z_out.at[rows], z_in.at[rows], z_send.at[0], z_recv.at[step], to_z)

    levels = (
        (CORES, core, own_0, near_0, near_core),
        (ZL, zl, own_1, near_1, near_z),
        (Y, y, own_2, near_2, near_y),
    )

    def spans(at, rows):
        return pl.ds(at * 2 // BS, rows * 2 // BS)

    def scan_start(level, slot, at, rows):
        _, _, own, near, peers = levels[level]
        here = spans(at, rows)
        for i, peer in enumerate(peers):
            remote(
                own.at[here], near.at[i, here], scan_send.at[level], scan_recv.at[level, slot], peer
            ).start()

    def scan_wait(level, slot, at, rows):
        _, _, _, near, peers = levels[level]
        whole = near.at[:, spans(at, rows)]
        remote(whole, whole, scan_send.at[level], scan_recv.at[level, slot], peers[0]).wait_recv()

    def scan_total(level, here):
        size, _, own, near, _ = levels[level]
        return sum((near[i, here] for i in range(size - 1)), own[here])

    def scan_part(level, here, lanes, later):
        size, mine, _, near, _ = levels[level]
        terms = []
        for i in range(size - 1):
            whose = (mine + size - 1 - i) % size
            counts = whose > mine if later else whose < mine
            terms.append(jnp.where(counts, near[i, here, lanes, :], 0.0))
        return sum(terms[1:], terms[0])

    def out_copy(at, rows, half):
        here = pl.ds(aligned(at + half * HALF_ROWS), rows)
        return pltpu.make_async_copy(out.at[here], out_hbm.at[here], out_sem.at[0])

    def place(step):
        return lax.rem(step, HALF) * PIECE

    def multiply(step, group, ready=None):
        x_a = (x + jnp.where(group == 0, 2, jnp.where(group == 3, 0, 1))) % X
        x_b = (x + jnp.where(group == 0, 2, jnp.where(group == 3, 0, 3))) % X
        cross = group == 1
        at = place(step)
        row_a = aligned(dest(step, x_a) + at + jnp.where(cross, HALF_ROWS, 0))
        row_b = aligned(dest(step, x_b) + at + jnp.where(cross, 0, HALF_ROWS))
        block_a, block_b = row_a // BS, row_b // BS
        blocks = (block_a, block_a + 1, block_b, block_b + 1)
        total = jnp.zeros((2 * PIECE, BS), F32)
        for pair in range(BLOCKS // 2):
            if ready is not None:
                ready(pair)
            coup = coups[2 * pair * PAIRS // SHARE]
            left = jnp.concatenate(
                [
                    jnp.concatenate([coup[table[2 * pair + k, block]] for k in range(2)], axis=1)
                    for block in blocks
                ],
                axis=0,
            )
            right = itv[pl.ds(pair * 2 * BS, 2 * BS), :]
            total = total + jnp.dot(left, right, preferred_element_type=F32)
        part[pl.ds(row_a, PIECE)] = total[:PIECE]
        part[pl.ds(row_b, PIECE)] = total[PIECE:]

    spread = (iota((POINTS, BS), 1) // SIDES == iota((POINTS, BS), 0)).astype(F32)
    sides = (iota((SIDES, BS), 1) % SIDES == iota((SIDES, BS), 0)).astype(F32)
    from_n, to_n = iota((BS, BS), 0), iota((BS, BS), 1)
    same_side = from_n % SIDES == to_n % SIDES
    upto = (same_side & (from_n // SIDES <= to_n // SIDES)).astype(F32)
    above = (same_side & (from_n // SIDES > to_n // SIDES)).astype(F32)

    def profile_row():
        return jnp.dot(prof[...], spread, precision=HIGH, preferred_element_type=F32)

    quad_step = 1.0 / math.sqrt(POINTS * Y * PLANE)

    def both(ref, at, rows):
        return jnp.concatenate(
            [ref[pl.ds(aligned(at), rows), :], ref[pl.ds(aligned(at + HALF_ROWS), rows), :]], axis=0
        )

    def expand(step):
        for half in range(2):
            here = pl.ds(pl.multiple_of(step * PIECE + half * HALF_ROWS, PIECE), PIECE)
            reg_e[here] = dot0(reg[:, here], spread)
            irr_e[here] = dot0(irr[:, here], spread)
            drv0[here] = dot0(diag[:, here], spread) * itv[here, :].astype(F32)

    def combine(step, at, rows):
        x_wait(0, step, at, rows)
        lo, hi = pl.ds(lower(step, at, x_next), rows), pl.ds(upper(step, at, x_last), rows)
        base = 2 * landed(step, at)
        part[lo] = part[lo] + relayed[pl.ds(aligned(base), rows)]
        x_start((4,), step, at, rows)
        part[hi] = part[hi] + relayed[pl.ds(aligned(base + rows), rows)]
        x_start((5,), step, at, rows)

    def own_sums(step, at, rows):
        x_wait(1, step, at, rows)
        base = 4 * landed(step, at)
        up_own, lo_own, lo_sum, up_sum = [
            arrived[pl.ds(aligned(base + i * rows), rows)] for i in range(4)
        ]
        lo = part[pl.ds(lower(step, at, x), rows)] + lo_own + lo_sum
        hi = part[pl.ds(upper(step, at, x), rows)] + up_own + up_sum
        return lo, hi

    def finish_far(step):
        lo, hi = own_sums(step, step * PIECE, PIECE)
        z_out[pl.ds(aligned(step * 2 * PIECE), PIECE)] = lo
        z_out[pl.ds(aligned(step * 2 * PIECE + PIECE), PIECE)] = hi
        z_copy(step).start()

    def finish_near(step, slot, at, rows, crossed):
        if crossed is not None:
            z_copy(crossed).wait_recv()
        lo, hi = own_sums(step, at, rows)
        base = at // PIECE * PIECE + at
        lo = lo + z_in[pl.ds(aligned(base), rows)]
        hi = hi + z_in[pl.ds(aligned(base + PIECE), rows)]
        coupled = jnp.concatenate([lo, hi], axis=0)
        driving = (both(drv0, at, rows) + profile_row() * coupled) * quad_step
        regular, irregular = both(reg_e, at, rows), both(irr_e, at, rows)
        outs, ins = regular * driving, irregular * driving
        totals = jnp.concatenate([dot1(sides, outs), dot1(sides, ins)], axis=0)
        for i in range(2 * rows // BS):
            own_0[at * 2 // BS + i] = totals[:, i * BS : (i + 1) * BS]
        scan_start(0, slot, at, rows)
        outward = jnp.dot(outs, upto, precision=HIGH, preferred_element_type=F32)
        inward = jnp.dot(ins, above, precision=HIGH, preferred_element_type=F32)
        result = both(src, at, rows).astype(F32) + irregular * outward + regular * inward
        local[pl.ds(aligned(at), rows)] = result[:rows]
        local[pl.ds(aligned(at + HALF_ROWS), rows)] = result[rows:]

    def chip_sum(slot, at, rows):
        scan_wait(0, slot, at, rows)
        own_1[spans(at, rows)] = scan_total(0, spans(at, rows))
        scan_start(1, slot, at, rows)

    def plane_sum(slot, at, rows):
        scan_wait(1, slot, at, rows)
        own_2[spans(at, rows)] = scan_total(1, spans(at, rows))
        scan_start(2, slot, at, rows)

    def emit(slot, at, rows):
        here = spans(at, rows)
        count = 2 * rows // BS

        sides_of = ((pl.ds(0, SIDES), False), (pl.ds(SIDES, SIDES), True))
        carries = [
            scan_part(0, here, lanes, later) + scan_part(1, here, lanes, later)
            for lanes, later in sides_of
        ]
        scan_wait(2, slot, at, rows)
        outward, inward = [
            jnp.concatenate([total[i] for i in range(count)], axis=1)
            for total in (
                carry + scan_part(2, here, lanes, later)
                for carry, (lanes, later) in zip(carries, sides_of)
            )
        ]
        updated = both(local, at, rows)
        updated = updated + both(irr_e, at, rows) * dot0(outward, sides)
        updated = updated + both(reg_e, at, rows) * dot0(inward, sides)
        updated = updated.astype(jnp.bfloat16)
        for half in range(2):
            out[pl.ds(aligned(at + half * HALF_ROWS), rows), :] = updated[half * rows : (half + 1) * rows]
            out_copy(at, rows, half).start()

    def regular_piece(call, piece):
        call(piece, piece * PIECE, PIECE)

    to_scalars.wait()
    loads[LOADS].wait()

    def ready(pair):
        if pair % (BLOCKS // 2 // LOADS) == 0:
            loads[pair // (BLOCKS // 2 // LOADS)].wait()

    multiply(0, 0, ready)
    for load in later_loads:
        load.start()
    pl.semaphore_wait(barrier, 3 + 1 + (ZL - 1) + (Y - 1))
    x_start((0, 1), 0, 0, PIECE)
    def first_groups(i, _):
        step = jnp.where((i == 0) | (i == 2) | (i == 8), 0, jnp.where(i < 5, 1, 2))
        group = jnp.where(i < 2, 1 - i, jnp.where(i < 5, i - jnp.where(i == 2, 0, 2), i - 5))
        multiply(step, group)

        @pl.when(i == 0)
        def _():
            x_start((2, 3), 0, 0, PIECE)

        @pl.when(i == 1)
        def _():
            x_start((0, 1), 1, PIECE, PIECE)

        @pl.when(i == 2)
        def _():
            combine(0, 0, PIECE)

        @pl.when(i == 3)
        def _():
            x_start((2, 3), 1, PIECE, PIECE)

        return 0

    lax.fori_loop(0, 9, first_groups, 0)
    for load in later_loads:
        load.wait()

    def one_step(step, _):
        at = place(step)
        x_start((0, 1), step, at, PIECE)
        combine(step - 1, place(step - 1), PIECE)
        x_start((2, 3), step, at, PIECE)

        @pl.when(step < HALF + 2)
        def _():
            finish_far(step - 2)

        @pl.when(step >= HALF + 2)
        def _():
            piece = step - HALF - 2
            finish_near(step - 2, piece, piece * PIECE, PIECE, piece)

        @pl.when(step >= HALF + 3)
        def _():
            regular_piece(plane_sum, step - HALF - 3)

        def one_group(group, _):
            multiply(jnp.where(group == 3, step - 1, step + 1), group)
            return 0

        lax.fori_loop(0, 4, one_group, 0)

        @pl.when(step < HALF + 2)
        def _():
            expand(step - 2)

        @pl.when(step >= HALF + 2)
        def _():
            regular_piece(chip_sum, step - HALF - 2)

        @pl.when(step >= HALF + 3)
        def _():
            regular_piece(emit, step - HALF - 3)

        return 0

    lax.fori_loop(2, STEPS - 1, one_step, 0)

    last = STEPS - 1

    def send(kinds, i):
        x_start(kinds, last + i, *TAIL[i])

    def meet(i):
        combine(last + i, *TAIL[i])

    def finish(i):
        finish_near(last + i, HALF - 1 + i, *TAIL[i], HALF - 1 if i == 0 else None)

    def finish_regular(piece):
        finish_near(HALF + piece, piece, piece * PIECE, PIECE, piece)

    def small_piece(call, i):
        call(HALF - 1 + i, *TAIL[i])

    send((0, 1), 0)
    combine(last - 1, (HALF - 2) * PIECE, PIECE)
    send((2, 3), 0)
    send((0, 1), 1)
    send((2, 3), 1)
    send((0, 1), 2)
    finish_regular(3)
    regular_piece(plane_sum, 2)
    meet(0)
    send((2, 3), 2)
    regular_piece(chip_sum, 3)

    def own_group(step, _):
        multiply(step, 3)
        return 0

    lax.fori_loop(last - 1, last + 1, own_group, 0)
    meet(1)
    meet(2)
    regular_piece(emit, 2)
    finish_regular(4)
    regular_piece(plane_sum, 3)
    finish(0)
    regular_piece(chip_sum, 4)
    small_piece(chip_sum, 0)
    finish(1)
    finish(2)
    small_piece(chip_sum, 1)
    small_piece(chip_sum, 2)
    regular_piece(emit, 3)
    regular_piece(plane_sum, 4)
    small_piece(plane_sum, 0)
    small_piece(plane_sum, 1)
    small_piece(plane_sum, 2)
    regular_piece(emit, 4)
    for i in range(len(TAIL)):
        small_piece(emit, i)

    for kind in range(6):
        whole = part.at[pl.ds(0, CHANNELS)]
        remote(whole, whole, x_send.at[kind], x_recv.at[0, 0], to_next).wait_send()
    remote(z_out, z_in, z_send.at[0], z_recv.at[0], to_z).wait_send()
    for level, (_, _, _, near, peers) in enumerate(levels):
        remote(near, near, scan_send.at[level], scan_recv.at[level, 0], peers[0]).wait_send()
    pltpu.make_async_copy(out, out_hbm, out_sem.at[0]).wait()


def per_device(iterate, source, coupling, pair_rows, diag_pot, profile, regular, irregular):
    anywhere = pl.BlockSpec(memory_space=pl.ANY)
    wide = pltpu.VMEM((CHANNELS, BS), F32)
    whole = pltpu.VMEM((CHANNELS, BS), jnp.bfloat16)
    narrow = pltpu.VMEM((POINTS, CHANNELS), F32)
    def tiles(*count):
        return pltpu.VMEM((*count, CHANNELS // BS, 2 * SIDES, BS), F32)

    share = pltpu.VMEM((SHARE + 1, BS, BS), jnp.bfloat16)
    dma = pltpu.SemaphoreType.DMA
    result = jax.ShapeDtypeStruct((CHANNELS, BS), jnp.bfloat16)
    updated = pl.pallas_call(
        sweep,
        out_shape=result,
        in_specs=[pl.BlockSpec(memory_space=pltpu.VMEM)] + [anywhere] * 7,
        out_specs=anywhere,
        scratch_shapes=[
            pltpu.VMEM((BS, BS), jnp.int32),
            pltpu.VMEM((1, POINTS), F32),
            pltpu.VMEM((BLOCKS, 2 * BS), jnp.int32),
            pltpu.SMEM((BLOCKS, 2 * BS), jnp.int32),
            share, share, share, share,
            whole, whole, narrow, narrow, narrow, whole,
            pltpu.VMEM((ROW_BLOCKS * BS, BS), F32),
            pltpu.VMEM((2 * CHANNELS, BS), F32),
            pltpu.VMEM((4 * CHANNELS, BS), F32),
            wide, wide, wide, wide, wide, wide,
            tiles(), tiles(), tiles(), tiles(CORES - 1), tiles(ZL - 1), tiles(Y - 1),
            dma((LOADS + 7,)), dma((1,)),
            dma((6,)), dma((2, SENDS)),
            dma((1,)), dma((HALF,)),
            dma((3,)), dma((3, HALF - 1 + len(TAIL))),
        ],
        compiler_params=pltpu.CompilerParams(
            collective_id=0, has_side_effects=True, vmem_limit_bytes=60 * 2**20
        ),
        name="sweep",
    )(
        pair_rows.T,
        coupling.reshape(BLOCKS * PAIRS, BS, BS),
        iterate,
        source,
        diag_pot.T,
        profile.reshape(1, POINTS),
        regular.T,
        irregular.T,
    )
    return updated


def solution(mesh):
    placed = (
        P("chan", "slab"),
        P("chan", "slab"),
        P("chan", None, None, None),
        P("chan", None),
        P("chan", "slab"),
        P("slab"),
        P("chan", "slab"),
        P("chan", "slab"),
    )
    return jax.shard_map(
        per_device, mesh=mesh, in_specs=placed, out_specs=P("chan", "slab"), check_vma=False
    )
```

```python
import math

import jax
import jax.numpy as jnp
from jax import lax
from jax.experimental import pallas as pl
from jax.experimental.pallas import tpu as pltpu
from jax.sharding import PartitionSpec as P

Y, ZL, CORES, ZH, X = 4, 4, 2, 2, 4
PLANE = ZL * CORES
BS = 128
BLOCKS = 24
PAIRS = 12
ROW_BLOCKS = 192
POINTS = 16
SIDES = 8
CHANNELS = BLOCKS * BS
HALF_ROWS = CHANNELS // 2
STEPS = 12
HALF = 6
PIECE = 256
MIX = 1
TAIL = ((1280, 128), (1408, 64), (1472, 64))
SENDS = STEPS - 1 + len(TAIL)
LOADS = 4
SHARE = BLOCKS * PAIRS // LOADS
HIGH = lax.Precision.HIGHEST
MESH = pl.DeviceIdType.MESH
F32 = jnp.float32


def dot0(a, b):
    return lax.dot_general(a, b, (((0,), (0,)), ((), ())), precision=HIGH, preferred_element_type=F32)


def dot1(a, b):
    return lax.dot_general(a, b, (((1,), (1,)), ((), ())), precision=HIGH, preferred_element_type=F32)


def iota(shape, dim):
    return lax.broadcasted_iota(jnp.int32, shape, dim)


def sweep(
    pairs, coup_hbm, iter_hbm, src_hbm, diag_hbm, prof_hbm, reg_hbm, irr_hbm, out_hbm,
    square, prof, table_v, table, coup_0, coup_1, coup_2, coup_3, itv, src, diag, reg, irr, out,
    part, relayed, arrived, z_out, z_in, crossed,
    drv0, reg_e, irr_e, local, own_0, own_1, own_2, near_0, near_1, near_2,
    in_sem, out_sem, x_send, x_recv, z_send, z_recv, cross_send, cross_recv,
    scan_send, scan_recv,
):
    slab = lax.axis_index("slab")
    chan = lax.axis_index("chan")
    y = slab // PLANE
    spot = slab % PLANE
    zl, core = spot // CORES, spot % CORES
    zh = chan // X
    x = chan % X
    x_next, x_last, x_over = (x + 1) % X, (x + 3) % X, (x + 2) % X
    to_next = {"chan": zh * X + x_next}
    to_last = {"chan": zh * X + x_last}
    to_z = {"chan": (1 - zh) * X + x}
    near_core = [{"slab": slab + 1 - 2 * core}]
    near_z = [{"slab": y * PLANE + (zl + hop) % ZL * CORES + core} for hop in range(1, ZL)]
    near_y = [{"slab": (y + hop) % Y * PLANE + spot} for hop in range(1, Y)]

    coups = (coup_0, coup_1, coup_2, coup_3)
    loads = [
        pltpu.make_async_copy(
            coup_hbm.at[pl.ds(i * SHARE, SHARE)], coups[i].at[pl.ds(0, SHARE)], in_sem.at[i]
        )
        for i in range(LOADS)
    ] + [
        pltpu.make_async_copy(given, held, in_sem.at[LOADS + i])
        for i, (given, held) in enumerate(
            ((iter_hbm, itv), (diag_hbm, diag), (reg_hbm, reg), (irr_hbm, irr), (src_hbm, src))
        )
    ]
    prof_load = pltpu.make_async_copy(prof_hbm, prof, in_sem.at[LOADS + 6])
    first_loads, later_loads = loads[: LOADS + 1], loads[LOADS + 1 :] + [prof_load]
    loads[LOADS].start()
    for load in loads[:LOADS]:
        load.start()

    barrier = pltpu.get_barrier_semaphore()
    for peer in (to_next, to_last, to_z):
        pl.semaphore_signal(barrier, inc=1, device_id=peer, device_id_type=MESH)
    for peer in near_core + near_z + near_y:
        pl.semaphore_signal(barrier, inc=1, device_id=peer, device_id_type=MESH)

    shape = (BLOCKS, 2 * BS)
    found = jnp.full(shape, SHARE, jnp.int32)
    square[:PAIRS, :BLOCKS] = pairs[...]
    named = square[...].T
    for p in range(PAIRS):
        found = jnp.where(named[:BLOCKS, p : p + 1] == iota(shape, 1), iota(shape, 0) % (SHARE // PAIRS) * PAIRS + p, found)
    table_v[...] = found
    to_scalars = pltpu.make_async_copy(table_v, table, in_sem.at[LOADS + 5])
    to_scalars.start()
    for coup in coups:
        coup[SHARE] = jnp.zeros((BS, BS), jnp.bfloat16)

    def aligned(row):
        return pl.multiple_of(row, 64)

    def dest(step, x_of):
        z_of = jnp.where(step < HALF, 1 - zh, zh)
        return (z_of * X + x_of) * CHANNELS

    def lower(step, at, x_of):
        return aligned(dest(step, x_of) + at)

    def upper(step, at, x_of):
        return aligned(dest(step, x_of) + at + HALF_ROWS)

    def landed(step, at):
        return jnp.where(step < HALF, 0, HALF_ROWS) + at

    def remote(src_ref, dst_ref, send, recv, peer):
        return pltpu.make_async_remote_copy(
            src_ref=src_ref, dst_ref=dst_ref, send_sem=send, recv_sem=recv,
            device_id=peer, device_id_type=MESH,
        )

    def x_copy(kind, step, at, rows):
        src_row, peer = (
            (lower(step, at, x_over), to_next),
            (upper(step, at, x_over), to_last),
            (upper(step, at, x_next), to_next),
            (lower(step, at, x_last), to_last),
            (lower(step, at, x_next), to_next),
            (upper(step, at, x_last), to_last),
        )[kind]
        if kind < 2:
            landing, first = relayed, 2 * landed(step, at) + kind * rows
        else:
            landing, first = arrived, 4 * landed(step, at) + (kind - 2) * rows
        return remote(
            part.at[pl.ds(src_row, rows)], landing.at[pl.ds(aligned(first), rows)],
            x_send.at[kind], x_recv.at[0 if kind < 2 else 1, step], peer,
        )

    def x_start(kinds, step, at, rows):
        for kind in kinds:
            x_copy(kind, step, at, rows).start()

    def x_wait(place, step, at, rows):
        landing, count = ((relayed, 2), (arrived, 4))[place]
        whole = landing.at[pl.ds(aligned(count * landed(step, at)), count * rows)]
        remote(whole, whole, x_send.at[0], x_recv.at[place, step], to_next).wait_recv()

    def z_copy(step):
        rows = pl.ds(aligned(step * 2 * PIECE), 2 * PIECE)
        return remote(z_out.at[rows], z_in.at[rows], z_send.at[0], z_recv.at[step], to_z)

    def cross_copy(side, step):
        src_row = (lower(step, step * PIECE, x_next), upper(step, step * PIECE, x_last))[side]
        return remote(
            part.at[pl.ds(src_row, PIECE)],
            crossed.at[pl.ds(aligned((2 * step + side) * PIECE), PIECE)],
            cross_send.at[0], cross_recv.at[step], to_z,
        )

    levels = (
        (CORES, core, own_0, near_0, near_core),
        (ZL, zl, own_1, near_1, near_z),
        (Y, y, own_2, near_2, near_y),
    )

    def spans(at, rows):
        return pl.ds(at * 2 // BS, rows * 2 // BS)

    def scan_start(level, slot, at, rows):
        _, _, own, near, peers = levels[level]
        here = spans(at, rows)
        for i, peer in enumerate(peers):
            remote(
                own.at[here], near.at[i, here], scan_send.at[level], scan_recv.at[level, slot], peer
            ).start()

    def scan_wait(level, slot, at, rows):
        _, _, _, near, peers = levels[level]
        whole = near.at[:, spans(at, rows)]
        remote(whole, whole, scan_send.at[level], scan_recv.at[level, slot], peers[0]).wait_recv()

    def scan_total(level, here):
        size, _, own, near, _ = levels[level]
        return sum((near[i, here] for i in range(size - 1)), own[here])

    def scan_part(level, here, lanes, later):
        size, mine, _, near, _ = levels[level]
        terms = []
        for i in range(size - 1):
            whose = (mine + size - 1 - i) % size
            counts = whose > mine if later else whose < mine
            terms.append(jnp.where(counts, near[i, here, lanes, :], 0.0))
        return sum(terms[1:], terms[0])

    def out_copy(at, rows, half):
        here = pl.ds(aligned(at + half * HALF_ROWS), rows)
        return pltpu.make_async_copy(out.at[here], out_hbm.at[here], out_sem.at[0])

    def place(step):
        return lax.rem(step, HALF) * PIECE

    def multiply(step, group, ready=None):
        x_a = (x + jnp.where(group == 0, 2, jnp.where(group == 3, 0, 1))) % X
        x_b = (x + jnp.where(group == 0, 2, jnp.where(group == 3, 0, 3))) % X
        cross = group == 1
        at = place(step)
        row_a = aligned(dest(step, x_a) + at + jnp.where(cross, HALF_ROWS, 0))
        row_b = aligned(dest(step, x_b) + at + jnp.where(cross, 0, HALF_ROWS))
        block_a, block_b = row_a // BS, row_b // BS
        blocks = (block_a, block_a + 1, block_b, block_b + 1)
        total = jnp.zeros((2 * PIECE, BS), F32)
        for pair in range(BLOCKS // 2):
            if ready is not None:
                ready(pair)
            coup = coups[2 * pair * PAIRS // SHARE]
            left = jnp.concatenate(
                [
                    jnp.concatenate([coup[table[2 * pair + k, block]] for k in range(2)], axis=1)
                    for block in blocks
                ],
                axis=0,
            )
            right = itv[pl.ds(pair * 2 * BS, 2 * BS), :]
            total = total + jnp.dot(left, right, preferred_element_type=F32)
        part[pl.ds(row_a, PIECE)] = total[:PIECE]
        part[pl.ds(row_b, PIECE)] = total[PIECE:]

    spread = (iota((POINTS, BS), 1) // SIDES == iota((POINTS, BS), 0)).astype(F32)
    sides = (iota((SIDES, BS), 1) % SIDES == iota((SIDES, BS), 0)).astype(F32)
    from_n, to_n = iota((BS, BS), 0), iota((BS, BS), 1)
    same_side = from_n % SIDES == to_n % SIDES
    upto = (same_side & (from_n // SIDES <= to_n // SIDES)).astype(F32)
    above = (same_side & (from_n // SIDES > to_n // SIDES)).astype(F32)

    def profile_row():
        return jnp.dot(prof[...], spread, precision=HIGH, preferred_element_type=F32)

    quad_step = 1.0 / math.sqrt(POINTS * Y * PLANE)

    def both(ref, at, rows):
        return jnp.concatenate(
            [ref[pl.ds(aligned(at), rows), :], ref[pl.ds(aligned(at + HALF_ROWS), rows), :]], axis=0
        )

    def expand(step):
        for half in range(2):
            here = pl.ds(pl.multiple_of(step * PIECE + half * HALF_ROWS, PIECE), PIECE)
            reg_e[here] = dot0(reg[:, here], spread)
            irr_e[here] = dot0(irr[:, here], spread)
            drv0[here] = dot0(diag[:, here], spread) * itv[here, :].astype(F32)

    def combine(step, at, rows):
        x_wait(0, step, at, rows)
        lo, hi = pl.ds(lower(step, at, x_next), rows), pl.ds(upper(step, at, x_last), rows)
        base = 2 * landed(step, at)
        part[lo] = part[lo] + relayed[pl.ds(aligned(base), rows)]
        part[hi] = part[hi] + relayed[pl.ds(aligned(base + rows), rows)]
        if rows < PIECE:
            x_start((4, 5), step, at, rows)
            return
        step = jnp.int32(step)

        @pl.when(step < MIX)
        def _():
            cross_copy(0, step).start()
            cross_copy(1, step).start()

        @pl.when((step >= HALF) & (step < HALF + MIX))
        def _():
            first = 2 * (step - HALF) * PIECE
            whole = crossed.at[pl.ds(aligned(first), 2 * PIECE)]
            remote(whole, whole, cross_send.at[0], cross_recv.at[step - HALF], to_z).wait_recv()
            part[lo] = part[lo] + crossed[pl.ds(aligned(first), PIECE)]
            part[hi] = part[hi] + crossed[pl.ds(aligned(first + PIECE), PIECE)]

        @pl.when(step >= MIX)
        def _():
            x_start((4, 5), step, at, rows)

    def own_sums(step, at, rows, summed=True):
        count = 4 if summed else 2
        base = 4 * landed(step, at)
        whole = arrived.at[pl.ds(aligned(base), count * rows)]
        remote(whole, whole, x_send.at[0], x_recv.at[1, step], to_next).wait_recv()
        come = [arrived[pl.ds(aligned(base + i * rows), rows)] for i in range(count)]
        lo = part[pl.ds(lower(step, at, x), rows)] + come[1]
        hi = part[pl.ds(upper(step, at, x), rows)] + come[0]
        if summed:
            lo, hi = lo + come[2], hi + come[3]
        return lo, hi

    def finish_far(step):
        def put(summed):
            lo, hi = own_sums(step, step * PIECE, PIECE, summed)
            z_out[pl.ds(aligned(step * 2 * PIECE), PIECE)] = lo
            z_out[pl.ds(aligned(step * 2 * PIECE + PIECE), PIECE)] = hi

        @pl.when(step < MIX)
        def _():
            put(False)

        @pl.when(step >= MIX)
        def _():
            put(True)

        z_copy(step).start()

    def finish_near(step, slot, at, rows, crossed):
        if crossed is not None:
            z_copy(crossed).wait_recv()
        lo, hi = own_sums(step, at, rows)
        base = at // PIECE * PIECE + at
        lo = lo + z_in[pl.ds(aligned(base), rows)]
        hi = hi + z_in[pl.ds(aligned(base + PIECE), rows)]
        coupled = jnp.concatenate([lo, hi], axis=0)
        driving = (both(drv0, at, rows) + profile_row() * coupled) * quad_step
        regular, irregular = both(reg_e, at, rows), both(irr_e, at, rows)
        outs, ins = regular * driving, irregular * driving
        totals = jnp.concatenate([dot1(sides, outs), dot1(sides, ins)], axis=0)
        for i in range(2 * rows // BS):
            own_0[at * 2 // BS + i] = totals[:, i * BS : (i + 1) * BS]
        scan_start(0, slot, at, rows)
        outward = jnp.dot(outs, upto, precision=HIGH, preferred_element_type=F32)
        inward = jnp.dot(ins, above, precision=HIGH, preferred_element_type=F32)
        result = both(src, at, rows).astype(F32) + irregular * outward + regular * inward
        local[pl.ds(aligned(at), rows)] = result[:rows]
        local[pl.ds(aligned(at + HALF_ROWS), rows)] = result[rows:]

    def chip_sum(slot, at, rows):
        scan_wait(0, slot, at, rows)
        own_1[spans(at, rows)] = scan_total(0, spans(at, rows))
        scan_start(1, slot, at, rows)

    def plane_sum(slot, at, rows):
        scan_wait(1, slot, at, rows)
        own_2[spans(at, rows)] = scan_total(1, spans(at, rows))
        scan_start(2, slot, at, rows)

    def emit(slot, at, rows):
        here = spans(at, rows)
        count = 2 * rows // BS

        sides_of = ((pl.ds(0, SIDES), False), (pl.ds(SIDES, SIDES), True))
        carries = [
            scan_part(0, here, lanes, later) + scan_part(1, here, lanes, later)
            for lanes, later in sides_of
        ]
        scan_wait(2, slot, at, rows)
        outward, inward = [
            jnp.concatenate([total[i] for i in range(count)], axis=1)
            for total in (
                carry + scan_part(2, here, lanes, later)
                for carry, (lanes, later) in zip(carries, sides_of)
            )
        ]
        updated = both(local, at, rows)
        updated = updated + both(irr_e, at, rows) * dot0(outward, sides)
        updated = updated + both(reg_e, at, rows) * dot0(inward, sides)
        updated = updated.astype(jnp.bfloat16)
        for half in range(2):
            out[pl.ds(aligned(at + half * HALF_ROWS), rows), :] = updated[half * rows : (half + 1) * rows]
            out_copy(at, rows, half).start()

    def regular_piece(call, piece):
        call(piece, piece * PIECE, PIECE)

    to_scalars.wait()
    loads[LOADS].wait()

    def ready(pair):
        if pair % (BLOCKS // 2 // LOADS) == 0:
            loads[pair // (BLOCKS // 2 // LOADS)].wait()

    multiply(0, 0, ready)
    for load in later_loads:
        load.start()
    pl.semaphore_wait(barrier, 3 + 1 + (ZL - 1) + (Y - 1))
    x_start((0, 1), 0, 0, PIECE)
    def first_groups(i, _):
        step = jnp.where((i == 0) | (i == 2) | (i == 8), 0, jnp.where(i < 5, 1, 2))
        group = jnp.where(i < 2, 1 - i, jnp.where(i < 5, i - jnp.where(i == 2, 0, 2), i - 5))
        multiply(step, group)

        @pl.when(i == 0)
        def _():
            x_start((2, 3), 0, 0, PIECE)

        @pl.when(i == 1)
        def _():
            x_start((0, 1), 1, PIECE, PIECE)

        @pl.when(i == 2)
        def _():
            combine(0, 0, PIECE)

        @pl.when(i == 3)
        def _():
            x_start((2, 3), 1, PIECE, PIECE)

        return 0

    lax.fori_loop(0, 9, first_groups, 0)
    for load in later_loads:
        load.wait()

    def one_step(step, _):
        at = place(step)
        x_start((0, 1), step, at, PIECE)
        combine(step - 1, place(step - 1), PIECE)
        x_start((2, 3), step, at, PIECE)

        @pl.when(step < HALF + 2)
        def _():
            finish_far(step - 2)

        @pl.when(step >= HALF + 2)
        def _():
            piece = step - HALF - 2
            finish_near(step - 2, piece, piece * PIECE, PIECE, piece)

        def one_group(group, _):
            multiply(jnp.where(group == 3, step - 1, step + 1), group)
            return 0

        lax.fori_loop(0, 4, one_group, 0)

        @pl.when(step < HALF + 2)
        def _():
            expand(step - 2)

        @pl.when(step >= HALF + 3)
        def _():
            regular_piece(chip_sum, step - HALF - 3)

        return 0

    lax.fori_loop(2, STEPS - 1, one_step, 0)

    last = STEPS - 1

    def send(kinds, i):
        x_start(kinds, last + i, *TAIL[i])

    def meet(i):
        combine(last + i, *TAIL[i])

    def finish(i):
        finish_near(last + i, HALF - 1 + i, *TAIL[i], HALF - 1 if i == 0 else None)

    def finish_regular(piece):
        finish_near(HALF + piece, piece, piece * PIECE, PIECE, piece)

    def small_piece(call, i):
        call(HALF - 1 + i, *TAIL[i])

    send((0, 1), 0)
    combine(last - 1, (HALF - 2) * PIECE, PIECE)
    send((2, 3), 0)
    send((0, 1), 1)
    send((2, 3), 1)
    send((0, 1), 2)
    finish_regular(3)
    meet(0)
    send((2, 3), 2)
    regular_piece(chip_sum, 2)

    def own_group(step, _):
        multiply(step, 3)
        return 0

    lax.fori_loop(last - 1, last + 1, own_group, 0)
    meet(1)
    meet(2)
    regular_piece(plane_sum, 0)
    regular_piece(chip_sum, 3)
    finish_regular(4)
    regular_piece(plane_sum, 1)
    finish(0)
    regular_piece(chip_sum, 4)
    small_piece(chip_sum, 0)
    finish(1)
    finish(2)
    small_piece(chip_sum, 1)
    regular_piece(plane_sum, 2)
    regular_piece(plane_sum, 3)
    small_piece(chip_sum, 2)
    regular_piece(emit, 0)
    regular_piece(emit, 1)
    regular_piece(plane_sum, 4)
    small_piece(plane_sum, 0)
    small_piece(plane_sum, 1)
    small_piece(plane_sum, 2)
    regular_piece(emit, 2)
    regular_piece(emit, 3)
    regular_piece(emit, 4)
    for i in range(len(TAIL)):
        small_piece(emit, i)

    for kind in range(6):
        whole = part.at[pl.ds(0, CHANNELS - (MIX * PIECE if kind > 3 else 0))]
        remote(whole, whole, x_send.at[kind], x_recv.at[0, 0], to_next).wait_send()
    remote(crossed, crossed, cross_send.at[0], cross_recv.at[0], to_z).wait_send()
    remote(z_out, z_in, z_send.at[0], z_recv.at[0], to_z).wait_send()
    for level, (_, _, _, near, peers) in enumerate(levels):
        remote(near, near, scan_send.at[level], scan_recv.at[level, 0], peers[0]).wait_send()
    pltpu.make_async_copy(out, out_hbm, out_sem.at[0]).wait()


def per_device(iterate, source, coupling, pair_rows, diag_pot, profile, regular, irregular):
    anywhere = pl.BlockSpec(memory_space=pl.ANY)
    wide = pltpu.VMEM((CHANNELS, BS), F32)
    whole = pltpu.VMEM((CHANNELS, BS), jnp.bfloat16)
    narrow = pltpu.VMEM((POINTS, CHANNELS), F32)
    def tiles(*count):
        return pltpu.VMEM((*count, CHANNELS // BS, 2 * SIDES, BS), F32)

    share = pltpu.VMEM((SHARE + 1, BS, BS), jnp.bfloat16)
    dma = pltpu.SemaphoreType.DMA
    result = jax.ShapeDtypeStruct((CHANNELS, BS), jnp.bfloat16)
    updated = pl.pallas_call(
        sweep,
        out_shape=result,
        in_specs=[pl.BlockSpec(memory_space=pltpu.VMEM)] + [anywhere] * 7,
        out_specs=anywhere,
        scratch_shapes=[
            pltpu.VMEM((BS, BS), jnp.int32),
            pltpu.VMEM((1, POINTS), F32),
            pltpu.VMEM((BLOCKS, 2 * BS), jnp.int32),
            pltpu.SMEM((BLOCKS, 2 * BS), jnp.int32),
            share, share, share, share,
            whole, whole, narrow, narrow, narrow, whole,
            pltpu.VMEM((ROW_BLOCKS * BS, BS), F32),
            pltpu.VMEM((2 * CHANNELS, BS), F32),
            pltpu.VMEM((4 * CHANNELS, BS), F32),
            wide, wide, pltpu.VMEM((2 * MIX * PIECE, BS), F32), wide, wide, wide, wide,
            tiles(), tiles(), tiles(), tiles(CORES - 1), tiles(ZL - 1), tiles(Y - 1),
            dma((LOADS + 7,)), dma((1,)),
            dma((6,)), dma((2, SENDS)),
            dma((1,)), dma((HALF,)), dma((1,)), dma((MIX,)),
            dma((3,)), dma((3, HALF - 1 + len(TAIL))),
        ],
        compiler_params=pltpu.CompilerParams(
            collective_id=0, has_side_effects=True, vmem_limit_bytes=60 * 2**20
        ),
        name="sweep",
    )(
        pair_rows.T,
        coupling.reshape(BLOCKS * PAIRS, BS, BS),
        iterate,
        source,
        diag_pot.T,
        profile.reshape(1, POINTS),
        regular.T,
        irregular.T,
    )
    return updated


def solution(mesh):
    placed = (
        P("chan", "slab"),
        P("chan", "slab"),
        P("chan", None, None, None),
        P("chan", None),
        P("chan", "slab"),
        P("slab"),
        P("chan", "slab"),
        P("chan", "slab"),
    )
    return jax.shard_map(
        per_device, mesh=mesh, in_specs=placed, out_specs=P("chan", "slab"), check_vma=False
    )
```

```python
import math

import jax
import jax.numpy as jnp
from jax import lax
from jax.experimental import pallas as pl
from jax.experimental.pallas import tpu as pltpu
from jax.sharding import PartitionSpec as P

Y, ZL, CORES, ZH, X = 4, 4, 2, 2, 4
PLANE = ZL * CORES
BS = 128
BLOCKS = 24
PAIRS = 12
ROW_BLOCKS = 192
POINTS = 16
SIDES = 8
CHANNELS = BLOCKS * BS
HALF_ROWS = CHANNELS // 2
STEPS = 12
HALF = 6
PIECE = 256
MIX = 1
TAIL = ((1280, 128), (1408, 128))
SENDS = STEPS - 1 + len(TAIL)
LOADS = 4
SHARE = BLOCKS * PAIRS // LOADS
HIGH = lax.Precision.HIGHEST
MESH = pl.DeviceIdType.MESH
F32 = jnp.float32


def dot0(a, b):
    return lax.dot_general(a, b, (((0,), (0,)), ((), ())), precision=HIGH, preferred_element_type=F32)


def dot1(a, b):
    return lax.dot_general(a, b, (((1,), (1,)), ((), ())), precision=HIGH, preferred_element_type=F32)


def iota(shape, dim):
    return lax.broadcasted_iota(jnp.int32, shape, dim)


def sweep(
    pairs_hbm, coup_hbm, iter_hbm, src_hbm, diag_hbm, prof_hbm, reg_hbm, irr_hbm, out_hbm,
    pairs, square, prof, table_v, table, coup_0, coup_1, coup_2, coup_3, itv, src, diag, reg, irr, out,
    part, relayed, arrived, z_out, z_in, crossed,
    drv0, reg_e, irr_e, local, own_0, own_1, own_2, near_0, near_1, near_2,
    in_sem, out_sem, x_send, x_recv, z_send, z_recv, cross_send, cross_recv,
    scan_send, scan_recv,
):
    slab = lax.axis_index("slab")
    chan = lax.axis_index("chan")
    y = slab // PLANE
    spot = slab % PLANE
    zl, core = spot // CORES, spot % CORES
    zh = chan // X
    x = chan % X
    x_next, x_last, x_over = (x + 1) % X, (x + 3) % X, (x + 2) % X
    to_next = {"chan": zh * X + x_next}
    to_last = {"chan": zh * X + x_last}
    to_z = {"chan": (1 - zh) * X + x}
    near_core = [{"slab": slab + 1 - 2 * core}]
    near_z = [{"slab": y * PLANE + (zl + hop) % ZL * CORES + core} for hop in range(1, ZL)]
    near_y = [{"slab": (y + hop) % Y * PLANE + spot} for hop in range(1, Y)]

    coups = (coup_0, coup_1, coup_2, coup_3)
    loads = [
        pltpu.make_async_copy(
            coup_hbm.at[pl.ds(i * SHARE, SHARE)], coups[i].at[pl.ds(0, SHARE)], in_sem.at[i]
        )
        for i in range(LOADS)
    ] + [
        pltpu.make_async_copy(given, held, in_sem.at[LOADS + i])
        for i, (given, held) in enumerate(
            ((iter_hbm, itv), (diag_hbm, diag), (reg_hbm, reg), (irr_hbm, irr), (src_hbm, src))
        )
    ]
    prof_load = pltpu.make_async_copy(prof_hbm, prof, in_sem.at[LOADS + 6])
    pairs_load = pltpu.make_async_copy(pairs_hbm, pairs, in_sem.at[LOADS + 7])
    pairs_load.start()
    first_loads, later_loads = loads[: LOADS + 1], loads[LOADS + 1 :] + [prof_load]
    loads[LOADS].start()
    for load in loads[:LOADS]:
        load.start()

    barrier = pltpu.get_barrier_semaphore()
    for peer in (to_next, to_last, to_z):
        pl.semaphore_signal(barrier, inc=1, device_id=peer, device_id_type=MESH)
    for peer in near_core + near_z + near_y:
        pl.semaphore_signal(barrier, inc=1, device_id=peer, device_id_type=MESH)

    shape = (BLOCKS, 2 * BS)
    found = jnp.full(shape, SHARE, jnp.int32)
    pairs_load.wait()
    square[:PAIRS, :BLOCKS] = pairs[...]
    named = square[...].T
    for p in range(PAIRS):
        found = jnp.where(named[:BLOCKS, p : p + 1] == iota(shape, 1), iota(shape, 0) % (SHARE // PAIRS) * PAIRS + p, found)
    table_v[...] = found
    to_scalars = pltpu.make_async_copy(table_v, table, in_sem.at[LOADS + 5])
    to_scalars.start()
    for coup in coups:
        coup[SHARE] = jnp.zeros((BS, BS), jnp.bfloat16)

    def aligned(row):
        return pl.multiple_of(row, 64)

    def dest(step, x_of):
        z_of = jnp.where(step < HALF, 1 - zh, zh)
        return (z_of * X + x_of) * CHANNELS

    def lower(step, at, x_of):
        return aligned(dest(step, x_of) + at)

    def upper(step, at, x_of):
        return aligned(dest(step, x_of) + at + HALF_ROWS)

    def landed(step, at):
        return jnp.where(step < HALF, 0, HALF_ROWS) + at

    def remote(src_ref, dst_ref, send, recv, peer):
        return pltpu.make_async_remote_copy(
            src_ref=src_ref, dst_ref=dst_ref, send_sem=send, recv_sem=recv,
            device_id=peer, device_id_type=MESH,
        )

    def x_copy(kind, step, at, rows):
        src_row, peer = (
            (lower(step, at, x_over), to_next),
            (upper(step, at, x_over), to_last),
            (upper(step, at, x_next), to_next),
            (lower(step, at, x_last), to_last),
            (lower(step, at, x_next), to_next),
            (upper(step, at, x_last), to_last),
        )[kind]
        if kind < 2:
            landing, first = relayed, 2 * landed(step, at) + kind * rows
        else:
            landing, first = arrived, 4 * landed(step, at) + (kind - 2) * rows
        return remote(
            part.at[pl.ds(src_row, rows)], landing.at[pl.ds(aligned(first), rows)],
            x_send.at[kind], x_recv.at[0 if kind < 2 else 1, step], peer,
        )

    def x_start(kinds, step, at, rows):
        for kind in kinds:
            x_copy(kind, step, at, rows).start()

    def x_wait(place, step, at, rows):
        landing, count = ((relayed, 2), (arrived, 4))[place]
        whole = landing.at[pl.ds(aligned(count * landed(step, at)), count * rows)]
        remote(whole, whole, x_send.at[0], x_recv.at[place, step], to_next).wait_recv()

    def z_copy(step):
        rows = pl.ds(aligned(step * 2 * PIECE), 2 * PIECE)
        return remote(z_out.at[rows], z_in.at[rows], z_send.at[0], z_recv.at[step], to_z)

    def cross_copy(side, step):
        src_row = (lower(step, step * PIECE, x_next), upper(step, step * PIECE, x_last))[side]
        return remote(
            part.at[pl.ds(src_row, PIECE)],
            crossed.at[pl.ds(aligned((2 * step + side) * PIECE), PIECE)],
            cross_send.at[0], cross_recv.at[step], to_z,
        )

    levels = (
        (CORES, core, own_0, near_0, near_core),
        (ZL, zl, own_1, near_1, near_z),
        (Y, y, own_2, near_2, near_y),
    )

    def spans(at, rows):
        return pl.ds(at * 2 // BS, rows * 2 // BS)

    def scan_start(level, slot, at, rows):
        _, _, own, near, peers = levels[level]
        here = spans(at, rows)
        for i, peer in enumerate(peers):
            remote(
                own.at[here], near.at[i, here], scan_send.at[level], scan_recv.at[level, slot], peer
            ).start()

    def scan_wait(level, slot, at, rows):
        _, _, _, near, peers = levels[level]
        whole = near.at[:, spans(at, rows)]
        remote(whole, whole, scan_send.at[level], scan_recv.at[level, slot], peers[0]).wait_recv()

    def scan_total(level, here):
        size, _, own, near, _ = levels[level]
        return sum((near[i, here] for i in range(size - 1)), own[here])

    def scan_part(level, here, lanes, later):
        size, mine, _, near, _ = levels[level]
        terms = []
        for i in range(size - 1):
            whose = (mine + size - 1 - i) % size
            counts = whose > mine if later else whose < mine
            terms.append(jnp.where(counts, near[i, here, lanes, :], 0.0))
        return sum(terms[1:], terms[0])

    def out_copy(at, rows, half):
        here = pl.ds(aligned(at + half * HALF_ROWS), rows)
        return pltpu.make_async_copy(out.at[here], out_hbm.at[here], out_sem.at[0])

    def place(step):
        return lax.rem(step, HALF) * PIECE

    def multiply(step, group, ready=None):
        x_a = (x + jnp.where(group == 0, 2, jnp.where(group == 3, 0, 1))) % X
        x_b = (x + jnp.where(group == 0, 2, jnp.where(group == 3, 0, 3))) % X
        cross = group == 1
        at = place(step)
        row_a = aligned(dest(step, x_a) + at + jnp.where(cross, HALF_ROWS, 0))
        row_b = aligned(dest(step, x_b) + at + jnp.where(cross, 0, HALF_ROWS))
        block_a, block_b = row_a // BS, row_b // BS
        blocks = (block_a, block_a + 1, block_b, block_b + 1)
        total = jnp.zeros((2 * PIECE, BS), F32)
        for pair in range(BLOCKS // 2):
            if ready is not None:
                ready(pair)
            coup = coups[2 * pair * PAIRS // SHARE]
            left = jnp.concatenate(
                [
                    jnp.concatenate([coup[table[2 * pair + k, block]] for k in range(2)], axis=1)
                    for block in blocks
                ],
                axis=0,
            )
            right = itv[pl.ds(pair * 2 * BS, 2 * BS), :]
            total = total + jnp.dot(left, right, preferred_element_type=F32)
        part[pl.ds(row_a, PIECE)] = total[:PIECE]
        part[pl.ds(row_b, PIECE)] = total[PIECE:]

    spread = (iota((POINTS, BS), 1) // SIDES == iota((POINTS, BS), 0)).astype(F32)
    sides = (iota((SIDES, BS), 1) % SIDES == iota((SIDES, BS), 0)).astype(F32)
    from_n, to_n = iota((BS, BS), 0), iota((BS, BS), 1)
    same_side = from_n % SIDES == to_n % SIDES
    upto = (same_side & (from_n // SIDES <= to_n // SIDES)).astype(F32)
    above = (same_side & (from_n // SIDES > to_n // SIDES)).astype(F32)

    def profile_row():
        return jnp.dot(prof[...], spread, precision=HIGH, preferred_element_type=F32)

    quad_step = 1.0 / math.sqrt(POINTS * Y * PLANE)

    def both(ref, at, rows):
        return jnp.concatenate(
            [ref[pl.ds(aligned(at), rows), :], ref[pl.ds(aligned(at + HALF_ROWS), rows), :]], axis=0
        )

    def expand(step):
        for half in range(2):
            here = pl.ds(pl.multiple_of(step * PIECE + half * HALF_ROWS, PIECE), PIECE)
            reg_e[here] = dot0(reg[:, here], spread)
            irr_e[here] = dot0(irr[:, here], spread)
            drv0[here] = dot0(diag[:, here], spread) * itv[here, :].astype(F32)

    def combine(step, at, rows):
        x_wait(0, step, at, rows)
        lo, hi = pl.ds(lower(step, at, x_next), rows), pl.ds(upper(step, at, x_last), rows)
        base = 2 * landed(step, at)
        part[lo] = part[lo] + relayed[pl.ds(aligned(base), rows)]
        part[hi] = part[hi] + relayed[pl.ds(aligned(base + rows), rows)]
        if rows < PIECE:
            x_start((4, 5), step, at, rows)
            return
        step = jnp.int32(step)

        @pl.when(step < MIX)
        def _():
            cross_copy(0, step).start()
            cross_copy(1, step).start()

        @pl.when((step >= HALF) & (step < HALF + MIX))
        def _():
            first = 2 * (step - HALF) * PIECE
            whole = crossed.at[pl.ds(aligned(first), 2 * PIECE)]
            remote(whole, whole, cross_send.at[0], cross_recv.at[step - HALF], to_z).wait_recv()
            part[lo] = part[lo] + crossed[pl.ds(aligned(first), PIECE)]
            part[hi] = part[hi] + crossed[pl.ds(aligned(first + PIECE), PIECE)]

        @pl.when(step >= MIX)
        def _():
            x_start((4, 5), step, at, rows)

    def own_sums(step, at, rows, summed=True):
        count = 4 if summed else 2
        base = 4 * landed(step, at)
        whole = arrived.at[pl.ds(aligned(base), count * rows)]
        remote(whole, whole, x_send.at[0], x_recv.at[1, step], to_next).wait_recv()
        come = [arrived[pl.ds(aligned(base + i * rows), rows)] for i in range(count)]
        lo = part[pl.ds(lower(step, at, x), rows)] + come[1]
        hi = part[pl.ds(upper(step, at, x), rows)] + come[0]
        if summed:
            lo, hi = lo + come[2], hi + come[3]
        return lo, hi

    def finish_far(step):
        def put(summed):
            lo, hi = own_sums(step, step * PIECE, PIECE, summed)
            z_out[pl.ds(aligned(step * 2 * PIECE), PIECE)] = lo
            z_out[pl.ds(aligned(step * 2 * PIECE + PIECE), PIECE)] = hi

        @pl.when(step < MIX)
        def _():
            put(False)

        @pl.when(step >= MIX)
        def _():
            put(True)

        z_copy(step).start()

    def finish_near(step, slot, at, rows, crossed):
        if crossed is not None:
            z_copy(crossed).wait_recv()
        lo, hi = own_sums(step, at, rows)
        base = at // PIECE * PIECE + at
        lo = lo + z_in[pl.ds(aligned(base), rows)]
        hi = hi + z_in[pl.ds(aligned(base + PIECE), rows)]
        coupled = jnp.concatenate([lo, hi], axis=0)
        driving = (both(drv0, at, rows) + profile_row() * coupled) * quad_step
        regular, irregular = both(reg_e, at, rows), both(irr_e, at, rows)
        outs, ins = regular * driving, irregular * driving
        totals = jnp.concatenate([dot1(sides, outs), dot1(sides, ins)], axis=0)
        for i in range(2 * rows // BS):
            own_0[at * 2 // BS + i] = totals[:, i * BS : (i + 1) * BS]
        scan_start(0, slot, at, rows)
        outward = jnp.dot(outs, upto, precision=HIGH, preferred_element_type=F32)
        inward = jnp.dot(ins, above, precision=HIGH, preferred_element_type=F32)
        result = both(src, at, rows).astype(F32) + irregular * outward + regular * inward
        local[pl.ds(aligned(at), rows)] = result[:rows]
        local[pl.ds(aligned(at + HALF_ROWS), rows)] = result[rows:]

    def chip_sum(slot, at, rows):
        scan_wait(0, slot, at, rows)
        own_1[spans(at, rows)] = scan_total(0, spans(at, rows))
        scan_start(1, slot, at, rows)

    def plane_sum(slot, at, rows):
        scan_wait(1, slot, at, rows)
        own_2[spans(at, rows)] = scan_total(1, spans(at, rows))
        scan_start(2, slot, at, rows)

    def emit(slot, at, rows):
        here = spans(at, rows)
        count = 2 * rows // BS

        sides_of = ((pl.ds(0, SIDES), False), (pl.ds(SIDES, SIDES), True))
        carries = [
            scan_part(0, here, lanes, later) + scan_part(1, here, lanes, later)
            for lanes, later in sides_of
        ]
        scan_wait(2, slot, at, rows)
        outward, inward = [
            jnp.concatenate([total[i] for i in range(count)], axis=1)
            for total in (
                carry + scan_part(2, here, lanes, later)
                for carry, (lanes, later) in zip(carries, sides_of)
            )
        ]
        updated = both(local, at, rows)
        updated = updated + both(irr_e, at, rows) * dot0(outward, sides)
        updated = updated + both(reg_e, at, rows) * dot0(inward, sides)
        updated = updated.astype(jnp.bfloat16)
        for half in range(2):
            out[pl.ds(aligned(at + half * HALF_ROWS), rows), :] = updated[half * rows : (half + 1) * rows]
            out_copy(at, rows, half).start()

    def regular_piece(call, piece):
        call(piece, piece * PIECE, PIECE)

    to_scalars.wait()
    loads[LOADS].wait()

    def ready(pair):
        if pair % (BLOCKS // 2 // LOADS) == 0:
            loads[pair // (BLOCKS // 2 // LOADS)].wait()

    multiply(0, 0, ready)
    for load in later_loads:
        load.start()
    pl.semaphore_wait(barrier, 3 + 1 + (ZL - 1) + (Y - 1))
    x_start((0, 1), 0, 0, PIECE)
    def first_groups(i, _):
        step = jnp.where((i == 0) | (i == 2) | (i == 8), 0, jnp.where(i < 5, 1, 2))
        group = jnp.where(i < 2, 1 - i, jnp.where(i < 5, i - jnp.where(i == 2, 0, 2), i - 5))
        multiply(step, group)

        @pl.when(i == 0)
        def _():
            x_start((2, 3), 0, 0, PIECE)

        @pl.when(i == 1)
        def _():
            x_start((0, 1), 1, PIECE, PIECE)

        @pl.when(i == 2)
        def _():
            combine(0, 0, PIECE)

        @pl.when(i == 3)
        def _():
            x_start((2, 3), 1, PIECE, PIECE)

        return 0

    lax.fori_loop(0, 9, first_groups, 0)
    for load in later_loads:
        load.wait()

    def one_step(step, _):
        at = place(step)
        x_start((0, 1), step, at, PIECE)
        x_start((2, 3), step, at, PIECE)
        combine(step - 1, place(step - 1), PIECE)

        @pl.when(step < HALF + 2)
        def _():
            finish_far(step - 2)

        @pl.when(step >= HALF + 2)
        def _():
            piece = step - HALF - 2
            finish_near(step - 2, piece, piece * PIECE, PIECE, piece)

        def one_group(group, _):
            multiply(jnp.where(group == 3, step - 1, step + 1), group)
            return 0

        lax.fori_loop(0, 4, one_group, 0)

        @pl.when(step < HALF + 2)
        def _():
            expand(step - 2)

        @pl.when(step >= HALF + 3)
        def _():
            regular_piece(chip_sum, step - HALF - 3)

        return 0

    lax.fori_loop(2, STEPS - 1, one_step, 0)

    last = STEPS - 1

    def send(kinds, i):
        x_start(kinds, last + i, *TAIL[i])

    def meet(i):
        combine(last + i, *TAIL[i])

    def finish(i):
        finish_near(last + i, HALF - 1 + i, *TAIL[i], HALF - 1 if i == 0 else None)

    def finish_regular(piece):
        finish_near(HALF + piece, piece, piece * PIECE, PIECE, piece)

    def small_piece(call, i):
        call(HALF - 1 + i, *TAIL[i])

    for i in range(len(TAIL)):
        send((0, 1), i)
    combine(last - 1, (HALF - 2) * PIECE, PIECE)
    for i in range(len(TAIL)):
        send((2, 3), i)
    finish_regular(3)
    meet(0)
    regular_piece(chip_sum, 2)

    def own_group(step, _):
        multiply(step, 3)
        return 0

    lax.fori_loop(last - 1, last + 1, own_group, 0)
    meet(1)
    regular_piece(chip_sum, 3)
    regular_piece(plane_sum, 0)
    finish_regular(4)
    regular_piece(plane_sum, 1)
    regular_piece(emit, 0)
    finish(0)
    regular_piece(chip_sum, 4)
    small_piece(chip_sum, 0)
    finish(1)
    small_piece(chip_sum, 1)
    regular_piece(plane_sum, 2)
    regular_piece(plane_sum, 3)
    regular_piece(emit, 1)
    regular_piece(plane_sum, 4)
    for i in range(len(TAIL)):
        small_piece(plane_sum, i)
    regular_piece(emit, 2)
    regular_piece(emit, 3)
    regular_piece(emit, 4)
    for i in range(len(TAIL)):
        small_piece(emit, i)

    for kind in range(6):
        whole = part.at[pl.ds(0, CHANNELS - (MIX * PIECE if kind > 3 else 0))]
        remote(whole, whole, x_send.at[kind], x_recv.at[0, 0], to_next).wait_send()
    remote(crossed, crossed, cross_send.at[0], cross_recv.at[0], to_z).wait_send()
    remote(z_out, z_in, z_send.at[0], z_recv.at[0], to_z).wait_send()
    for level, (_, _, _, near, peers) in enumerate(levels):
        remote(near, near, scan_send.at[level], scan_recv.at[level, 0], peers[0]).wait_send()
    pltpu.make_async_copy(out, out_hbm, out_sem.at[0]).wait()


def per_device(iterate, source, coupling, pair_rows, diag_pot, profile, regular, irregular):
    anywhere = pl.BlockSpec(memory_space=pl.ANY)
    wide = pltpu.VMEM((CHANNELS, BS), F32)
    whole = pltpu.VMEM((CHANNELS, BS), jnp.bfloat16)
    narrow = pltpu.VMEM((POINTS, CHANNELS), F32)
    def tiles(*count):
        return pltpu.VMEM((*count, CHANNELS // BS, 2 * SIDES, BS), F32)

    share = pltpu.VMEM((SHARE + 1, BS, BS), jnp.bfloat16)
    dma = pltpu.SemaphoreType.DMA
    result = jax.ShapeDtypeStruct((CHANNELS, BS), jnp.bfloat16)
    updated = pl.pallas_call(
        sweep,
        out_shape=result,
        in_specs=[anywhere] * 8,
        out_specs=anywhere,
        scratch_shapes=[
            pltpu.VMEM((PAIRS, BLOCKS), jnp.int32),
            pltpu.VMEM((BS, BS), jnp.int32),
            pltpu.VMEM((1, POINTS), F32),
            pltpu.VMEM((BLOCKS, 2 * BS), jnp.int32),
            pltpu.SMEM((BLOCKS, 2 * BS), jnp.int32),
            share, share, share, share,
            whole, whole, narrow, narrow, narrow, whole,
            pltpu.VMEM((ROW_BLOCKS * BS, BS), F32),
            pltpu.VMEM((2 * CHANNELS, BS), F32),
            pltpu.VMEM((4 * CHANNELS, BS), F32),
            wide, wide, pltpu.VMEM((2 * MIX * PIECE, BS), F32), wide, wide, wide, wide,
            tiles(), tiles(), tiles(), tiles(CORES - 1), tiles(ZL - 1), tiles(Y - 1),
            dma((LOADS + 8,)), dma((1,)),
            dma((6,)), dma((2, SENDS)),
            dma((1,)), dma((HALF,)), dma((1,)), dma((MIX,)),
            dma((3,)), dma((3, HALF - 1 + len(TAIL))),
        ],
        compiler_params=pltpu.CompilerParams(
            collective_id=0, has_side_effects=True, vmem_limit_bytes=60 * 2**20
        ),
        name="sweep",
    )(
        pair_rows.T,
        coupling.reshape(BLOCKS * PAIRS, BS, BS),
        iterate,
        source,
        diag_pot.T,
        profile.reshape(1, POINTS),
        regular.T,
        irregular.T,
    )
    return updated


def solution(mesh):
    placed = (
        P("chan", "slab"),
        P("chan", "slab"),
        P("chan", None, None, None),
        P("chan", None),
        P("chan", "slab"),
        P("slab"),
        P("chan", "slab"),
        P("chan", "slab"),
    )
    return jax.shard_map(
        per_device, mesh=mesh, in_specs=placed, out_specs=P("chan", "slab"), check_vma=False
    )
```
